32 devices in a mesh: groups: 2 (over x), brick: 16 (over z, y, core).
Axes of the slice: x: 2, y: 2, z: 4, core: 2. Of those that a mesh axis runs over, the one named last changes fastest.
Arguments:
- point_features: bfloat16 [32, 131072], P(None, ('groups', 'brick')), parts along dimension 1, may hold values from -6 to 6
- point_positions: float32 [3, 131072], P(None, ('groups', 'brick')), parts along dimension 1, may hold values from -1 to 128, as said below
- owner_brick: int32 [1024], P(('groups', 'brick')), parts along dimension 0, may hold values from 0 to 15, as said below
- block_rows: int32 [1024, 4], P(('groups', 'brick')), parts along dimension 0, may hold values from 0 to 1023, as said below
- mode_scale: float32 [32, 32, 32, 64], P(None, None, 'brick'), may hold values from -8 to 8
- channel_mix: float32 [32, 32], replicated, may hold values from -1 to 1
- skip_weight: bfloat16 [32, 32], replicated, may hold values from -1 to 1
- cotangent: bfloat16 [32, 256, 128, 128], P(None, ('groups', 'brick')), parts along dimension 1, may hold values from -6 to 6
Outputs:
- latent_grid: bfloat16 [32, 256, 128, 128], P(None, ('groups', 'brick')), parts along dimension 1
- point_grads: bfloat16 [32, 131072], P(None, ('groups', 'brick')), parts along dimension 1
- mix_grads: float32 [64, 32], P('groups'), parts along dimension 0
The draws below stay inside these ranges and needn't reach their ends.
There are 2 independent parts, one for each index of `groups`. The reference program is written for one: setup_inputs(seed, part) draws one part's arguments, and reference() takes and returns one part's arrays. A program takes and returns all parts, laid end to end along the dimension named above; an argument that names none is the same for every part. Nothing has to cross between parts.
Inputs may be any that keep to these rules, and one draw needn't show every extreme that they name: `owner_brick`: of the 32 blocks of one brick's points, at most 6 share an owner; in every draw one brick owns exactly 6 blocks of every brick's points. `block_rows`: row = plane * 128 + y inside the owner's slab; a block's 4 rows share the plane and have consecutive y. `point_positions`: dimension 0 holds x, y, z. A block's points lie within half a cell in x of its rows' plane and within half a cell in y of its rows' span.
All inputs are finite; a program needn't handle non-finite values.
Results may differ from the reference program's by a relative error of at most 0.015.
Values may be sent and summed in bfloat16 or wider, within the bound.
A program may use at most 192 MiB of HBM per device.

```python
import math
import jax
import jax.numpy as jnp
from jax import lax

C = 32
G = 128
MODES = 32
NB = 4
P_SIZE = 65536
PB = 32
NBLK = 512
CAP = 6
XLOC = 8
N_BRICK = 16


def pick_owners(key):
    key = jax.random.fold_in(key, 101)
    key_crowd, key_level, key_noise, key_order = jax.random.split(key, 4)
    crowded = jax.random.randint(key_crowd, (), 0, N_BRICK).astype(jnp.int32)
    levels = jax.random.randint(key_level, (N_BRICK,), 0, 3).astype(jnp.int32)
    entries = jnp.arange(N_BRICK * CAP, dtype=jnp.int32)
    entry_brick = entries // CAP
    noise = jax.random.randint(key_noise, (N_BRICK, N_BRICK * CAP), 0, 1024).astype(jnp.int32)
    scores = jnp.where(entry_brick[None, :] == crowded, -1, levels[entry_brick][None, :] * 1024 + noise)
    scores = scores * (N_BRICK * CAP) + entries[None, :]
    ranked = jnp.argsort(-scores, axis=1)
    chosen = entry_brick[ranked[:, :PB - CAP]]
    crowded_part = jnp.full((N_BRICK, CAP), crowded, jnp.int32)
    listed = jnp.concatenate([crowded_part, chosen], axis=1)
    shuffle = jax.random.randint(key_order, (N_BRICK, PB), 0, 1024).astype(jnp.int32) * PB + jnp.arange(PB, dtype=jnp.int32)[None, :]
    order = jnp.argsort(shuffle, axis=1)
    return jnp.take_along_axis(listed, order, axis=1).reshape(-1).astype(jnp.int32)


def pick_anchors(key):
    key = jax.random.fold_in(key, 202)
    key_plane, key_line = jax.random.split(key)
    plane = jax.random.randint(key_plane, (NBLK,), 0, XLOC).astype(jnp.int32)
    start = jax.random.randint(key_line, (NBLK,), 0, G - NB + 1).astype(jnp.int32)
    return (plane, start)


def draw_owner_brick(key, part):
    return pick_owners(key)


def draw_block_rows(key, part):
    plane, start = pick_anchors(key)
    return (plane[:, None] * G + start[:, None] + jnp.arange(NB, dtype=jnp.int32)[None, :]).astype(jnp.int32)


def draw_point_positions(key, part):
    owners = pick_owners(key)
    plane, start = pick_anchors(key)
    key = jax.random.fold_in(key, 3)
    spread = jax.random.uniform(key, (3, NBLK, 128), dtype=jnp.float32)
    across = (owners * XLOC + plane).astype(jnp.float32)[:, None] + spread[0] - 0.5
    along = start.astype(jnp.float32)[:, None] - 0.5 + spread[1] * NB
    depth = spread[2] * G
    return jnp.stack([across, along, depth]).reshape(3, NBLK * 128).astype(jnp.float32)


def block_scale(own_key, extent, cuts, low, high):
    def one(axis_at, parts):
        draws = jax.random.uniform(jax.random.fold_in(jax.random.fold_in(own_key, 6), axis_at), (parts,), jnp.float32, low / len(cuts), high / len(cuts))
        return jnp.repeat(jnp.exp(draws), extent[axis_at] // parts).reshape((-1,) + (1,) * (len(extent) - axis_at - 1))

    level = one(*cuts[0])
    for cut in cuts[1:]:
        level = level * one(*cut)
    return level


def gaussian(rng, dims, scale, reach, shards=(), kind=jnp.bfloat16):
    result = scale * jax.random.normal(rng, dims, jnp.float32)
    if shards:
        result = result * block_scale(rng, dims, shards, -0.22, 0.18)
    return jnp.clip(result, -reach, reach).astype(kind)


def setup_inputs(seed: int = 0, part: int = 0) -> dict:
    key_list = jax.random.split(jax.random.key(seed), 9)
    part_splits = jax.random.split(jax.random.fold_in(key_list[8], part), 9)
    point_features = gaussian(part_splits[0], (C, P_SIZE), 1.0, 6.0, ((1, 16),))
    point_positions = draw_point_positions(jax.random.fold_in(jax.random.fold_in(key_list[8], part), 71), part)
    owner_brick = draw_owner_brick(jax.random.fold_in(jax.random.fold_in(key_list[8], part), 71), part)
    block_rows = draw_block_rows(jax.random.fold_in(jax.random.fold_in(key_list[8], part), 71), part)
    mode_scale = gaussian(key_list[4], (C, MODES, MODES, 2 * MODES), 2.0, 8.0, ((2, 16),), jnp.float32)
    channel_mix = gaussian(key_list[5], (C, C), C ** -0.5, 1.0, (), jnp.float32)
    skip_weight = gaussian(key_list[6], (C, C), C ** -0.5, 1.0)
    cotangent = gaussian(part_splits[7], (C, G, G, G), 1.0, 6.0, ((1, 16),))
    return dict(point_features=point_features, point_positions=point_positions, owner_brick=owner_brick, block_rows=block_rows, mode_scale=mode_scale, channel_mix=channel_mix, skip_weight=skip_weight, cotangent=cotangent)


def spectral_tables(grid_size, mode_count):
    positions = jnp.arange(grid_size, dtype=jnp.int32)
    numbers = jnp.arange(mode_count, dtype=jnp.int32)
    signed = jnp.where(numbers < mode_count // 2, numbers, numbers - mode_count)
    multiple = positions[:, None] * signed[None, :] % grid_size
    angles = multiple.astype(jnp.float32) * (2.0 * math.pi / grid_size)
    cosine_table = jnp.cos(angles).astype(jnp.bfloat16)
    sine_table = jnp.sin(angles).astype(jnp.bfloat16)
    line_turns = positions[:, None] * numbers[None, :] % grid_size
    line_angles = line_turns.astype(jnp.float32) * (2.0 * math.pi / grid_size)
    line_table = jnp.stack([jnp.cos(line_angles), -jnp.sin(line_angles)], axis=-1)
    line_table = line_table.reshape(grid_size, 2 * mode_count).astype(jnp.bfloat16)
    return (cosine_table, sine_table, line_table)

def rotate(values, direction):
    paired = values.reshape(values.shape[:-1] + (values.shape[-1] // 2, 2))
    turned = jnp.stack([direction * paired[..., 1], -direction * paired[..., 0]], axis=-1)
    return turned.reshape(values.shape)

def product(pattern, operand, table):
    return jnp.einsum(pattern, operand.astype(jnp.float32), table.astype(jnp.float32), precision=lax.Precision.HIGHEST)

def fourier_section(pattern, values, cosine_table, sine_table, direction):
    return product(pattern, values, cosine_table) + rotate(product(pattern, values, sine_table), direction)

def complex_times(factor, values, conjugate):
    factor_pairs = factor.reshape(factor.shape[:-1] + (-1, 2))
    value_pairs = values.reshape(values.shape[:-1] + (-1, 2))
    factor_re = factor_pairs[..., 0]
    factor_im = factor_pairs[..., 1]
    value_re = value_pairs[..., 0]
    value_im = value_pairs[..., 1]
    if conjugate:
        real_part = factor_re * value_re + factor_im * value_im
        imag_part = factor_re * value_im - factor_im * value_re
    else:
        real_part = factor_re * value_re - factor_im * value_im
        imag_part = factor_re * value_im + factor_im * value_re
    return jnp.stack([real_part, imag_part], axis=-1).reshape(values.shape)

def kernels(places, row_across, row_along, grid_size):
    near_plane = jnp.exp(-0.5 * ((row_across[:, :, None] - places[0][:, None, :]) ** 2 + (row_along[:, :, None] - places[1][:, None, :]) ** 2))
    depths = jnp.arange(grid_size, dtype=jnp.float32)
    near_line = jnp.exp(-0.5 * (depths[None, :, None] - places[2][:, None, :]) ** 2).astype(jnp.bfloat16)
    return (near_plane, near_line)

def reference(point_features, point_positions, owner_brick, block_rows, mode_scale, channel_mix, skip_weight, cotangent):
    channels = point_features.shape[0]
    blocks = owner_brick.shape[0]
    slab_planes = G // N_BRICK
    features = point_features.reshape(channels, blocks, 128)
    places = point_positions.reshape(3, blocks, 128)
    row_across = owner_brick[:, None] * slab_planes + block_rows // G
    row_along = block_rows % G
    near_plane, near_line = kernels(places, row_across.astype(jnp.float32), row_along.astype(jnp.float32), G)
    weighted = (features[:, :, None, :].astype(jnp.float32) * near_plane[None]).astype(jnp.bfloat16)
    contribution = product('cbjp,bzp->cbjz', weighted, near_line)
    flat_rows = (row_across * G + row_along).reshape(-1).astype(jnp.int32)
    summed = jnp.zeros((channels, G * G, G), jnp.float32).at[:, flat_rows, :].add(contribution.reshape(channels, -1, G))
    encoded = summed.reshape(channels, G, G, G).astype(jnp.bfloat16)
    cosine_table, sine_table, line_table = spectral_tables(G, MODES)
    cell_share = 1.0 / (G * G * G)
    z_modes = product('cxyz,zr->cxyr', encoded, line_table).astype(jnp.bfloat16)
    y_modes = fourier_section('cxyr,yk->cxkr', z_modes, cosine_table, sine_table, 1.0).astype(jnp.bfloat16)
    modes = fourier_section('cxkr,xj->cjkr', y_modes, cosine_table, sine_table, 1.0)
    scaled = complex_times(mode_scale, modes, False)
    mixed_modes = product('dc,cjkr->djkr', channel_mix, scaled).astype(jnp.bfloat16)
    back_x = fourier_section('cjkr,xj->cxkr', mixed_modes, cosine_table, sine_table, -1.0).astype(jnp.bfloat16)
    back_y = fourier_section('cxkr,yk->cxyr', back_x, cosine_table, sine_table, -1.0).astype(jnp.bfloat16)
    spectral = product('cxyr,zr->cxyz', back_y, line_table) * cell_share
    pre_act = spectral + product('dc,cxyz->dxyz', skip_weight, encoded)
    latent_grid = jax.nn.gelu(pre_act).astype(jnp.bfloat16)
    _, gelu_back = jax.vjp(jax.nn.gelu, pre_act)
    grad_pre = gelu_back(cotangent.astype(jnp.float32))[0].astype(jnp.bfloat16)
    grad_zmodes = (product('cxyz,zr->cxyr', grad_pre, line_table) * cell_share).astype(jnp.bfloat16)
    grad_ymodes = fourier_section('cxyr,yk->cxkr', grad_zmodes, cosine_table, sine_table, 1.0).astype(jnp.bfloat16)
    grad_modes = fourier_section('cxkr,xj->cjkr', grad_ymodes, cosine_table, sine_table, 1.0)
    mix_grads = product('djkr,cjkr->dc', grad_modes, scaled) / G
    grad_scaled = product('dc,djkr->cjkr', channel_mix, grad_modes)
    grad_spec = complex_times(mode_scale, grad_scaled, True).astype(jnp.bfloat16)
    grad_back_x = fourier_section('cjkr,xj->cxkr', grad_spec, cosine_table, sine_table, -1.0).astype(jnp.bfloat16)
    grad_back_y = fourier_section('cxkr,yk->cxyr', grad_back_x, cosine_table, sine_table, -1.0).astype(jnp.bfloat16)
    grad_encoded = (product('cxyr,zr->cxyz', grad_back_y, line_table) + product('dc,dxyz->cxyz', skip_weight, grad_pre)).astype(jnp.bfloat16)
    rows_grad = grad_encoded.reshape(channels, G * G, G)[:, flat_rows, :].reshape(channels, blocks, -1, G)
    grad_near = product('cbjz,bzp->cbjp', rows_grad, near_line)
    point_grads = lax.optimization_barrier(jnp.sum(grad_near * near_plane[None], axis=2)).reshape(channels, -1).astype(jnp.bfloat16)
    return (latent_grid, point_grads, mix_grads)
```

```python
import math

import jax
import jax.numpy as jnp
import numpy as np
from jax import lax
from jax.experimental import pallas as pl
from jax.experimental.pallas import tpu as pltpu
from jax.sharding import PartitionSpec as P

F32 = jnp.float32
BF16 = jnp.bfloat16
VMEM_BYTES = 56 * 1024 * 1024


def rounded(values):
    return np.asarray(values, np.float32).astype(jnp.bfloat16).astype(np.float32)


def tables(grid, modes, bricks, planes, own_modes):
    place = np.arange(grid)
    numbers = np.arange(modes)
    signed = np.where(numbers < modes // 2, numbers, numbers - modes)
    turns = (place[:, None] * signed[None, :] % grid) * (2.0 * math.pi / grid)
    cosine, sine = rounded(np.cos(turns)), rounded(np.sin(turns))
    line_turns = (place[:, None] * numbers[None, :] % grid) * (2.0 * math.pi / grid)
    line = np.stack([np.cos(line_turns), -np.sin(line_turns)], axis=-1)
    line = rounded(line.reshape(grid, 2 * modes))
    turn = np.zeros((2 * modes, 2 * modes), np.float32)
    turn[2 * numbers + 1, 2 * numbers] = 1.0
    turn[2 * numbers, 2 * numbers + 1] = -1.0
    two = np.eye(2, dtype=np.float32)
    z_in = np.concatenate([np.kron(two, line), np.kron(two, line @ turn)], axis=1)
    y_in = np.concatenate([cosine.T, sine.T], axis=1)
    z_out = np.concatenate([np.kron(two, line.T), np.kron(two, turn @ line.T)], axis=1)
    y_out = np.concatenate([cosine, -sine], axis=1)
    x_in = np.zeros((2, own_modes, modes, bricks, own_modes, planes), np.float32)
    x_out = np.zeros((bricks, own_modes, planes, 2, own_modes, modes), np.float32)
    by_brick_cos = cosine.reshape(bricks, planes, modes)
    by_brick_sin = sine.reshape(bricks, planes, modes)
    for k in range(own_modes):
        x_in[0, k, :, :, k, :] = by_brick_cos.transpose(2, 0, 1)
        x_in[1, k, :, :, k, :] = by_brick_sin.transpose(2, 0, 1)
        x_out[:, k, :, 0, k, :] = by_brick_cos
        x_out[:, k, :, 1, k, :] = -by_brick_sin
    rows = bricks * own_modes * planes
    x_in = x_in.reshape(2 * own_modes * modes, rows)
    x_out = x_out.reshape(rows, 2 * own_modes * modes)
    return z_in, y_in, z_out, y_out, x_in, x_out


def dot(left, right):
    return jnp.dot(left, right, preferred_element_type=F32)


def is_even(shape):
    return lax.broadcasted_iota(jnp.int32, shape, 1) % 2 == 0


def rotate(values, even):
    return jnp.where(even, pltpu.roll(values, 127, 1), -pltpu.roll(values, 1, 1))


def near_rows(block):
    dx = block[32:33] + block[33:34]
    dy = block[34:35] + block[35:36]
    return [jnp.exp(-0.5 * (dx * dx + (dy + float(j)) * (dy + float(j)))) for j in range(4)]


def near_line_of(block, grid):
    depth = lax.broadcasted_iota(jnp.int32, (grid, 128), 0).astype(F32)
    away = (depth - block[36:37]) - (block[37:38] + block[38:39])
    return jnp.exp(-0.5 * away * away).astype(BF16)


def forward_lines(first, second, z_in, y_in):
    pair = jnp.concatenate([first.astype(BF16), second.astype(BF16)], axis=1)
    both = dot(pair, z_in).astype(BF16)
    return dot(y_in, jnp.concatenate([both[:, :128], both[:, 128:]], axis=0))


def inverse_lines(values, z_out, y_out):
    both = dot(values.astype(BF16), z_out).astype(BF16)
    return dot(y_out, jnp.concatenate([both[:, :256], both[:, 256:]], axis=0))


def encode_kernel(capacity, planes, grid, base, got, z_in, y_in, encoded, y_modes, total, held):
    x = pl.program_id(0)
    channels = got.shape[1] - 8
    line_rows = grid * channels
    modes = y_in.shape[0]
    exchange_rows = modes * planes

    @pl.when(x == 0)
    def _():
        @pl.loop(0, total.shape[0] // 512)
        def _(i):
            total[pl.ds(pl.multiple_of(i * 512, 512), 512), :] = jnp.zeros((512, 128), F32)

        @pl.loop(0, got.shape[0] // capacity)
        def _(i):
            sums = []
            for s in range(capacity):
                block = got[i * capacity + s].astype(F32)
                weighted = jnp.concatenate(
                    [(block[:channels] * near).astype(BF16) for near in near_rows(block)], axis=0
                )
                sums.append(
                    lax.dot_general(
                        weighted,
                        near_line_of(block, grid),
                        (((1,), (1,)), ((), ())),
                        preferred_element_type=F32,
                    )
                )
            for s in range(capacity):
                start = pl.multiple_of(base[i * capacity + s] * channels, channels)
                total[pl.ds(start, 4 * channels), :] += sums[s]

    start = pl.multiple_of(x * line_rows, line_rows)
    encoded[...] = total[pl.ds(start, line_rows), :].astype(BF16)

    for p in range(channels // 2):
        out = forward_lines(
            total[pl.ds(start + 2 * p, grid, stride=channels), :],
            total[pl.ds(start + 2 * p + 1, grid, stride=channels), :],
            z_in[...],
            y_in[...],
        )
        held[pl.ds(p * exchange_rows + x, modes, stride=planes), :] = out

    @pl.when(x == planes - 1)
    def _():
        for p in range(channels // 2):
            y_modes[:, p * 128 : (p + 1) * 128] = held[
                p * exchange_rows : (p + 1) * exchange_rows, :
            ].astype(BF16)


def x_forward(got, x_in, even, rows):
    both = dot(x_in[...], got[...])
    parts = []
    for p in range(got.shape[1] // 128):
        span = slice(p * 128, (p + 1) * 128)
        parts.append(both[:rows, span] + rotate(both[rows:, span], even))
    return parts


def scale_parts(scale, even):
    real = jnp.where(even, scale, pltpu.roll(scale, 1, 1))
    imag = jnp.where(even, pltpu.roll(scale, 127, 1), scale)
    return real, imag


def mix_pairs(d, weights, straight, swapped, pairs):
    total = weights[d, 0:1, :] * straight[0] + weights[d, 1:2, :] * swapped[0]
    for p in range(1, pairs):
        total += weights[d, 2 * p : 2 * p + 1, :] * straight[p]
        total += weights[d, 2 * p + 1 : 2 * p + 2, :] * swapped[p]
    return total


def middle_kernel(got, x_in, x_out, scale, weights, scaled, back, straight, swapped):
    rows = scale.shape[0]
    pairs = got.shape[1] // 128
    even = is_even((rows, 128))
    for p, modes in enumerate(x_forward(got, x_in, even, rows)):
        span = slice(p * 128, (p + 1) * 128)
        real, imag = scale_parts(scale[:, span], even)
        value = modes * real - rotate(modes, even) * imag
        scaled[:, span] = value
        straight[p] = value
        swapped[p] = pltpu.roll(value, 64, 1)
    for d in range(pairs):
        mixed = mix_pairs(d, weights, straight, swapped, pairs)
        stacked = jnp.concatenate([mixed, rotate(mixed, even)], axis=0).astype(BF16)
        back[:, d * 128 : (d + 1) * 128] = dot(x_out[...], stacked).astype(BF16)


def middle_grad_kernel(
    got, x_in, x_out, scale, weights, scaled, back, products, straight, swapped
):
    rows = scale.shape[0]
    pairs = got.shape[1] // 128
    even = is_even((rows, 128))
    for p, grad in enumerate(x_forward(got, x_in, even, rows)):
        straight[p] = grad
        swapped[p] = pltpu.roll(grad, 64, 1)
    for c in range(pairs):
        span = slice(c * 128, (c + 1) * 128)
        mixed = mix_pairs(c, weights, straight, swapped, pairs)
        real, imag = scale_parts(scale[:, span], even)
        value = mixed * real + rotate(mixed, even) * imag
        stacked = jnp.concatenate([value, rotate(value, even)], axis=0).astype(BF16)
        back[:, span] = dot(x_out[...], stacked).astype(BF16)
    for c in range(pairs):
        value = scaled[:, c * 128 : (c + 1) * 128]
        for d in range(pairs):
            at = (c * pairs + d) * 2
            products[at : at + 1, :] = jnp.sum(value * straight[d], axis=0, keepdims=True)
            products[at + 1 : at + 2, :] = jnp.sum(value * swapped[d], axis=0, keepdims=True)


def spread(got, held):
    rows = got.shape[0]
    for p in range(got.shape[1] // 128):
        held[p * rows : (p + 1) * rows, :] = got[:, p * 128 : (p + 1) * 128].astype(F32)


def layer_kernel(
    planes,
    got,
    encoded,
    cotangent,
    skip,
    z_out,
    y_out,
    z_in,
    y_in,
    latent,
    grad_rows,
    y_modes,
    held,
    skipped,
    grads,
    held_out,
):
    x = pl.program_id(0)
    channels, grid = cotangent.shape[0], cotangent.shape[2]
    modes = y_in.shape[0]
    exchange_rows = modes * planes

    @pl.when(x == 0)
    def _():
        spread(got, held)

    for g in range(grid * channels // 256):
        skipped[g * 256 : (g + 1) * 256, :] = dot(skip[...], encoded[g * 256 : (g + 1) * 256, :])

    root = math.sqrt(2.0 / math.pi)

    @pl.loop(0, channels // 2)
    def _(p):
        values = held[pl.ds(p * exchange_rows + x, modes, stride=planes), :]
        spectral = inverse_lines(values, z_out[...], y_out[...])
        halves = []
        for h in range(2):
            d = 2 * p + h
            pre = spectral[:, h * 128 : (h + 1) * 128] + skipped[pl.ds(d, grid, stride=channels), :]
            square = pre * pre
            turned = jnp.tanh(pre * (root + (root * 0.044715) * square))
            gate = 0.5 + 0.5 * turned
            latent[d, 0] = (pre * gate).astype(BF16)
            slope = gate + (0.5 * pre) * (1.0 - turned * turned) * (
                root + (root * 3.0 * 0.044715) * square
            )
            grad = cotangent[d, 0].astype(F32) * slope
            grads[pl.ds(d, grid, stride=channels), :] = grad
            halves.append(grad)
        held_out[pl.ds(p * exchange_rows + x, modes, stride=planes), :] = forward_lines(
            halves[0], halves[1], z_in[...], y_in[...]
        )

    grad_rows[...] = grads[...].astype(BF16)

    @pl.when(x == planes - 1)
    def _():
        for p in range(channels // 2):
            y_modes[:, p * 128 : (p + 1) * 128] = held_out[
                p * exchange_rows : (p + 1) * exchange_rows, :
            ].astype(BF16)


def pull_kernel(
    capacity,
    planes,
    grid,
    base,
    got,
    back,
    grad_rows,
    skip,
    z_out,
    y_out,
    point_grads,
    held,
    rows_held,
    total,
    arrived,
):
    channels = point_grads.shape[1]
    exchange_rows = back.shape[0]
    modes = exchange_rows // planes
    copy = pltpu.make_async_copy(grad_rows, rows_held, arrived)
    copy.start()
    spread(back, held)

    @pl.loop(0, planes)
    def _(x):
        for p in range(channels // 2):
            values = held[pl.ds(p * exchange_rows + x, modes, stride=planes), :]
            lines = inverse_lines(values, z_out[...], y_out[...])
            for h in range(2):
                start = x * (grid * channels) + 2 * p + h
                total[pl.ds(start, grid, stride=channels), :] = lines[:, h * 128 : (h + 1) * 128]

    copy.wait()

    @pl.loop(0, got.shape[0] // capacity)
    def _(i):
        for s in range(capacity):
            block = got[i * capacity + s].astype(F32)
            start = pl.multiple_of(base[i * capacity + s] * channels, channels)
            span = pl.ds(start, 4 * channels)
            rows = total[span, :] + dot(skip[...], rows_held[span, :])
            near = dot(rows.astype(BF16), near_line_of(block, grid))
            summed = jnp.zeros((channels, 128), F32)
            for j, weight in enumerate(near_rows(block)):
                summed += near[j * channels : (j + 1) * channels] * weight
            point_grads[i * capacity + s] = summed.astype(BF16)


def vmem():
    return pl.BlockSpec(memory_space=pltpu.VMEM)


def params(**more):
    return pltpu.CompilerParams(vmem_limit_bytes=VMEM_BYTES, **more)


def whole(shape):
    return pl.BlockSpec(shape, lambda x: (0,) * len(shape))


def pair_weights(mix):
    channels = mix.shape[0]
    pairs = channels // 2
    cut = mix.reshape(pairs, 2, pairs, 2)
    straight = jnp.stack([cut[:, 0, :, 0], cut[:, 1, :, 1]], axis=-1)
    swapped = jnp.stack([cut[:, 0, :, 1], cut[:, 1, :, 0]], axis=-1)
    both = jnp.stack([straight, swapped], axis=2).reshape(pairs, channels, 2)
    return jnp.repeat(both, 64, axis=-1)


def exchange(values):
    return lax.all_to_all(values, "brick", split_axis=0, concat_axis=0, tiled=True)


def shards(
    point_features,
    point_positions,
    owner_brick,
    block_rows,
    mode_scale,
    channel_mix,
    skip_weight,
    cotangent,
):
    channels, points = point_features.shape
    blocks = points // 128
    planes, grid = cotangent.shape[1], cotangent.shape[2]
    mode_count, own_modes = mode_scale.shape[1], mode_scale.shape[2]
    bricks = lax.axis_size("brick")
    capacity = 3 * blocks // bricks
    slots = bricks * capacity
    local_rows = planes * grid
    width = channels * 2 * mode_count
    exchange_rows = mode_count * planes
    line_rows = grid * channels
    pairs = channels // 2
    z_in, y_in, z_out, y_out, x_in, x_out = tables(grid, mode_count, bricks, planes, own_modes)
    share = 1.0 / (grid * grid * grid)

    member = (owner_brick[:, None] == jnp.arange(bricks, dtype=jnp.int32)[None, :]).astype(
        jnp.int32
    )
    earlier = jnp.cumsum(member, axis=0) - member
    target = owner_brick * capacity + jnp.sum(earlier * member, axis=1)
    chosen = (jnp.arange(slots, dtype=jnp.int32)[:, None] == target[None, :]).astype(BF16)
    first_row = jnp.min(block_rows, axis=1)
    plane, along = first_row // grid, first_row % grid
    places = point_positions.reshape(3, blocks, 128)
    dx = (owner_brick * planes + plane).astype(F32)[:, None] - places[0]
    dy = along.astype(F32)[:, None] - places[1]
    cell = jnp.round(places[2])
    dz = places[2] - cell

    def head(values):
        return lax.reduce_precision(values, 8, 7)

    lanes = jnp.arange(128, dtype=jnp.int32)[None, :]
    named = jnp.where(lanes < 64, plane[:, None], along[:, None]).astype(F32)
    extra = jnp.stack(
        [head(dx), dx - head(dx), head(dy), dy - head(dy), cell, head(dz), dz - head(dz), named],
        axis=1,
    ).astype(BF16)
    features = point_features.reshape(channels, blocks, 128).transpose(1, 0, 2)
    sent = jnp.concatenate([features, extra], axis=1)
    sent = jnp.einsum("sb,brp->srp", chosen, sent, preferred_element_type=F32).astype(BF16)
    got = exchange(sent)
    ids = got[:, channels + 7, :].astype(F32).astype(jnp.int32)
    base = jnp.clip(ids[:, 0] * grid + ids[:, 64], 0, local_rows - 4)

    table = lambda values: jnp.asarray(values, BF16)
    smem = pl.BlockSpec(memory_space=pltpu.SMEM)
    encoded, y_modes = pl.pallas_call(
        lambda *refs: encode_kernel(capacity, planes, grid, *refs),
        grid=(planes,),
        in_specs=[smem, whole(got.shape), whole(z_in.shape), whole(y_in.shape)],
        out_specs=[
            pl.BlockSpec((line_rows, 128), lambda x: (x, 0)),
            whole((exchange_rows, width)),
        ],
        out_shape=[
            jax.ShapeDtypeStruct((planes * line_rows, 128), BF16),
            jax.ShapeDtypeStruct((exchange_rows, width), BF16),
        ],
        scratch_shapes=[
            pltpu.VMEM((planes * line_rows, 128), F32),
            pltpu.VMEM((pairs * exchange_rows, 128), F32),
        ],
        compiler_params=params(),
        name="encode",
    )(base, got, table(z_in), table(y_in))

    scale = mode_scale.transpose(2, 1, 0, 3).reshape(own_modes * mode_count, width)
    held_modes = pltpu.VMEM((pairs, own_modes * mode_count, 128), F32)
    scaled, back = pl.pallas_call(
        middle_kernel,
        in_specs=[vmem()] * 5,
        out_specs=[vmem()] * 2,
        out_shape=[
            jax.ShapeDtypeStruct(scale.shape, F32),
            jax.ShapeDtypeStruct((exchange_rows, width), BF16),
        ],
        scratch_shapes=[held_modes, held_modes],
        compiler_params=params(),
        name="middle",
    )(exchange(y_modes), table(x_in), table(x_out), scale, pair_weights(channel_mix))

    eye8 = jnp.eye(256 // channels, dtype=BF16)
    eye4 = jnp.eye(4, dtype=BF16)
    planes_spec = pl.BlockSpec((channels, 1, grid, grid), lambda x: (0, x, 0, 0))
    rows_spec = pl.BlockSpec((line_rows, 128), lambda x: (x, 0))
    latent_grid, grad_rows, grad_y_modes = pl.pallas_call(
        lambda *refs: layer_kernel(planes, *refs),
        grid=(planes,),
        in_specs=[
            whole((exchange_rows, width)),
            rows_spec,
            planes_spec,
            whole((256, 256)),
            whole(z_out.shape),
            whole(y_out.shape),
            whole(z_in.shape),
            whole(y_in.shape),
        ],
        out_specs=[planes_spec, rows_spec, whole((exchange_rows, width))],
        out_shape=[
            jax.ShapeDtypeStruct(cotangent.shape, BF16),
            jax.ShapeDtypeStruct((planes * line_rows, 128), BF16),
            jax.ShapeDtypeStruct((exchange_rows, width), BF16),
        ],
        scratch_shapes=[
            pltpu.VMEM((pairs * exchange_rows, 128), F32),
            pltpu.VMEM((line_rows, 128), F32),
            pltpu.VMEM((line_rows, 128), F32),
            pltpu.VMEM((pairs * exchange_rows, 128), F32),
        ],
        compiler_params=params(),
        name="layer",
    )(
        exchange(back),
        encoded,
        cotangent,
        jnp.kron(eye8, skip_weight),
        table(z_out * share),
        table(y_out),
        table(z_in * share),
        table(y_in),
    )

    grad_back, products = pl.pallas_call(
        middle_grad_kernel,
        in_specs=[vmem()] * 6,
        out_specs=[vmem()] * 2,
        out_shape=[
            jax.ShapeDtypeStruct((exchange_rows, width), BF16),
            jax.ShapeDtypeStruct((2 * pairs * pairs, 128), F32),
        ],
        scratch_shapes=[held_modes, held_modes],
        compiler_params=params(),
        name="middle_grad",
    )(
        exchange(grad_y_modes),
        table(x_in),
        table(x_out),
        scale,
        pair_weights(channel_mix.T),
        scaled,
    )
    by_half = jnp.sum(products.reshape(pairs, pairs, 2, 2, 64), axis=-1)
    by_part = jnp.stack(
        [
            jnp.stack([by_half[:, :, 0, 0], by_half[:, :, 1, 0]], axis=-1),
            jnp.stack([by_half[:, :, 1, 1], by_half[:, :, 0, 1]], axis=-1),
        ],
        axis=2,
    )
    local_mix = by_part.transpose(1, 3, 0, 2).reshape(channels, channels)
    mix_grads = lax.psum(local_mix, "brick") / grid

    pulled = pl.pallas_call(
        lambda *refs: pull_kernel(capacity, planes, grid, *refs),
        in_specs=[smem, vmem(), vmem(), pl.BlockSpec(memory_space=pl.ANY)] + [vmem()] * 3,
        out_specs=vmem(),
        out_shape=jax.ShapeDtypeStruct((slots, channels, 128), BF16),
        scratch_shapes=[
            pltpu.VMEM((pairs * exchange_rows, 128), F32),
            pltpu.VMEM((planes * line_rows, 128), BF16),
            pltpu.VMEM((planes * line_rows, 128), F32),
            pltpu.SemaphoreType.DMA,
        ],
        compiler_params=params(),
        name="pull",
    )(
        base,
        got,
        exchange(grad_back),
        grad_rows,
        jnp.kron(eye4, skip_weight.T),
        table(z_out),
        table(y_out),
    )
    returned = exchange(pulled)
    point_grads = jnp.einsum("sb,scp->cbp", chosen, returned, preferred_element_type=F32)
    return (latent_grid, point_grads.astype(BF16).reshape(channels, points), mix_grads)


def solution(mesh):
    in_specs = (
        P(None, ("groups", "brick")),
        P(None, ("groups", "brick")),
        P(("groups", "brick")),
        P(("groups", "brick"), None),
        P(None, None, "brick", None),
        P(),
        P(),
        P(None, ("groups", "brick"), None, None),
    )
    out_specs = (
        P(None, ("groups", "brick"), None, None),
        P(None, ("groups", "brick")),
        P("groups", None),
    )
    return jax.shard_map(shards, mesh=mesh, in_specs=in_specs, out_specs=out_specs, check_vma=False)
```

```python
import math

import jax
import jax.numpy as jnp
import numpy as np
from jax import lax
from jax.experimental import pallas as pl
from jax.experimental.pallas import tpu as pltpu
from jax.sharding import PartitionSpec as P

F32 = jnp.float32
BF16 = jnp.bfloat16
VMEM_BYTES = 56 * 1024 * 1024


def rounded(values):
    return np.asarray(values, np.float32).astype(jnp.bfloat16).astype(np.float32)


def tables(grid, modes, bricks, planes, own_modes):
    place = np.arange(grid)
    numbers = np.arange(modes)
    signed = np.where(numbers < modes // 2, numbers, numbers - modes)
    turns = (place[:, None] * signed[None, :] % grid) * (2.0 * math.pi / grid)
    cosine, sine = rounded(np.cos(turns)), rounded(np.sin(turns))
    line_turns = (place[:, None] * numbers[None, :] % grid) * (2.0 * math.pi / grid)
    line = np.stack([np.cos(line_turns), -np.sin(line_turns)], axis=-1)
    line = rounded(line.reshape(grid, 2 * modes))
    turn = np.zeros((2 * modes, 2 * modes), np.float32)
    turn[2 * numbers + 1, 2 * numbers] = 1.0
    turn[2 * numbers, 2 * numbers + 1] = -1.0
    two = np.eye(2, dtype=np.float32)
    z_in = np.concatenate([np.kron(two, line), np.kron(two, line @ turn)], axis=1)
    y_in = np.concatenate([cosine.T, sine.T], axis=1)
    z_out = np.concatenate([np.kron(two, line.T), np.kron(two, turn @ line.T)], axis=1)
    y_out = np.concatenate([cosine, -sine], axis=1)
    x_in = np.zeros((2, own_modes, modes, bricks, own_modes, planes), np.float32)
    x_out = np.zeros((bricks, own_modes, planes, 2, own_modes, modes), np.float32)
    by_brick_cos = cosine.reshape(bricks, planes, modes)
    by_brick_sin = sine.reshape(bricks, planes, modes)
    for k in range(own_modes):
        x_in[0, k, :, :, k, :] = by_brick_cos.transpose(2, 0, 1)
        x_in[1, k, :, :, k, :] = by_brick_sin.transpose(2, 0, 1)
        x_out[:, k, :, 0, k, :] = by_brick_cos
        x_out[:, k, :, 1, k, :] = -by_brick_sin
    rows = bricks * own_modes * planes
    x_in = x_in.reshape(2 * own_modes * modes, rows)
    x_out = x_out.reshape(rows, 2 * own_modes * modes)
    return z_in, y_in, z_out, y_out, x_in, x_out


def dot(left, right):
    return jnp.dot(left, right, preferred_element_type=F32)


def is_even(shape):
    return lax.broadcasted_iota(jnp.int32, shape, 1) % 2 == 0


def rotate(values, even):
    return jnp.where(even, pltpu.roll(values, 127, 1), -pltpu.roll(values, 1, 1))


def near_rows(block):
    dx = block[32:33] + block[33:34]
    dy = block[34:35] + block[35:36]
    return [jnp.exp(-0.5 * (dx * dx + (dy + float(j)) * (dy + float(j)))) for j in range(4)]


def near_line_of(block, grid):
    depth = lax.broadcasted_iota(jnp.int32, (grid, 128), 0).astype(F32)
    away = (depth - block[36:37]) - (block[37:38] + block[38:39])
    return jnp.exp(-0.5 * away * away).astype(BF16)


def forward_lines(first, second, z_in, y_in):
    pair = jnp.concatenate([first.astype(BF16), second.astype(BF16)], axis=1)
    both = dot(pair, z_in).astype(BF16)
    return dot(y_in, jnp.concatenate([both[:, :128], both[:, 128:]], axis=0))


def inverse_lines(values, z_out, y_out):
    both = dot(values.astype(BF16), z_out).astype(BF16)
    return dot(y_out, jnp.concatenate([both[:, :256], both[:, 256:]], axis=0))


def encode_kernel(capacity, planes, grid, base, got, z_in, y_in, encoded, y_modes, total, held):
    x = pl.program_id(0)
    channels = got.shape[1] - 8
    pitch = channels + 8
    modes = y_in.shape[0]
    exchange_rows = modes * planes

    @pl.when(x == 0)
    def _():
        @pl.loop(0, total.shape[0] // 512)
        def _(i):
            total[pl.ds(pl.multiple_of(i * 512, 512), 512), :] = jnp.zeros((512, 128), F32)

        @pl.loop(0, got.shape[0] // capacity)
        def _(i):
            sums = []
            for s in range(capacity):
                block = got[i * capacity + s].astype(F32)
                weighted = jnp.concatenate(
                    [(block[:channels] * near).astype(BF16) for near in near_rows(block)], axis=0
                )
                sums.append(
                    lax.dot_general(
                        weighted,
                        near_line_of(block, grid),
                        (((1,), (1,)), ((), ())),
                        preferred_element_type=F32,
                    )
                )
            for s in range(capacity):
                for j in range(4):
                    start = pl.multiple_of((base[i * capacity + s] + j) * pitch, 8)
                    total[pl.ds(start, channels), :] += sums[s][j * channels : (j + 1) * channels]

    start = pl.multiple_of(x * (grid * pitch), 8)
    for y in range(grid):
        encoded[y * channels : (y + 1) * channels, :] = total[
            pl.ds(start + y * pitch, channels), :
        ].astype(BF16)

    for p in range(channels // 2):
        out = forward_lines(
            total[pl.ds(start + 2 * p, grid, stride=pitch), :],
            total[pl.ds(start + 2 * p + 1, grid, stride=pitch), :],
            z_in[...],
            y_in[...],
        )
        held[pl.ds(p * exchange_rows + x, modes, stride=planes), :] = out

    @pl.when(x == planes - 1)
    def _():
        for p in range(channels // 2):
            y_modes[:, p * 128 : (p + 1) * 128] = held[
                p * exchange_rows : (p + 1) * exchange_rows, :
            ].astype(BF16)


def x_forward(got, x_in, even, rows):
    both = dot(x_in[...], got[...])
    parts = []
    for p in range(got.shape[1] // 128):
        span = slice(p * 128, (p + 1) * 128)
        parts.append(both[:rows, span] + rotate(both[rows:, span], even))
    return parts


def scale_parts(scale, even):
    real = jnp.where(even, scale, pltpu.roll(scale, 1, 1))
    imag = jnp.where(even, pltpu.roll(scale, 127, 1), scale)
    return real, imag


def mix_pairs(d, weights, straight, swapped, pairs):
    total = weights[d, 0:1, :] * straight[0] + weights[d, 1:2, :] * swapped[0]
    for p in range(1, pairs):
        total += weights[d, 2 * p : 2 * p + 1, :] * straight[p]
        total += weights[d, 2 * p + 1 : 2 * p + 2, :] * swapped[p]
    return total


def middle_kernel(got, x_in, x_out, scale, weights, scaled, back, straight, swapped):
    rows = scale.shape[0]
    pairs = got.shape[1] // 128
    even = is_even((rows, 128))
    for p, modes in enumerate(x_forward(got, x_in, even, rows)):
        span = slice(p * 128, (p + 1) * 128)
        real, imag = scale_parts(scale[:, span], even)
        value = modes * real - rotate(modes, even) * imag
        scaled[:, span] = value
        straight[p] = value
        swapped[p] = pltpu.roll(value, 64, 1)
    for d in range(pairs):
        mixed = mix_pairs(d, weights, straight, swapped, pairs)
        stacked = jnp.concatenate([mixed, rotate(mixed, even)], axis=0).astype(BF16)
        back[:, d * 128 : (d + 1) * 128] = dot(x_out[...], stacked).astype(BF16)


def middle_grad_kernel(
    got, x_in, x_out, scale, weights, scaled, back, products, straight, swapped
):
    rows = scale.shape[0]
    pairs = got.shape[1] // 128
    even = is_even((rows, 128))
    for p, grad in enumerate(x_forward(got, x_in, even, rows)):
        straight[p] = grad
        swapped[p] = pltpu.roll(grad, 64, 1)
    for c in range(pairs):
        span = slice(c * 128, (c + 1) * 128)
        mixed = mix_pairs(c, weights, straight, swapped, pairs)
        real, imag = scale_parts(scale[:, span], even)
        value = mixed * real + rotate(mixed, even) * imag
        stacked = jnp.concatenate([value, rotate(value, even)], axis=0).astype(BF16)
        back[:, span] = dot(x_out[...], stacked).astype(BF16)
    for c in range(pairs):
        value = scaled[:, c * 128 : (c + 1) * 128]
        for d in range(pairs):
            at = (c * pairs + d) * 2
            products[at : at + 1, :] = jnp.sum(value * straight[d], axis=0, keepdims=True)
            products[at + 1 : at + 2, :] = jnp.sum(value * swapped[d], axis=0, keepdims=True)


def spread(got, held):
    rows = got.shape[0]
    for p in range(got.shape[1] // 128):
        held[p * rows : (p + 1) * rows, :] = got[:, p * 128 : (p + 1) * 128].astype(F32)


def layer_kernel(
    planes,
    got,
    encoded,
    cotangent,
    skip,
    z_out,
    y_out,
    z_in,
    y_in,
    latent,
    grad_rows,
    y_modes,
    held,
    skipped,
    pre_act,
    grads,
    held_out,
):
    x = pl.program_id(0)
    channels, grid = cotangent.shape[0], cotangent.shape[2]
    pitch = channels + 8
    modes = y_in.shape[0]
    exchange_rows = modes * planes

    @pl.when(x == 0)
    def _():
        spread(got, held)

    for g in range(grid * channels // 256):
        mixed = dot(skip[...], encoded[g * 256 : (g + 1) * 256, :])
        for i in range(256 // channels):
            y = g * (256 // channels) + i
            skipped[y * pitch : y * pitch + channels, :] = mixed[i * channels : (i + 1) * channels]

    root = math.sqrt(2.0 / math.pi)

    for p in range(channels // 2):
        values = held[pl.ds(p * exchange_rows + x, modes, stride=planes), :]
        spectral = inverse_lines(values, z_out[...], y_out[...])
        for h in range(2):
            d = 2 * p + h
            mixed = skipped[pl.ds(d, grid, stride=pitch), :]
            pre_act[d] = spectral[:, h * 128 : (h + 1) * 128] + mixed

    @pl.loop(0, channels, unroll=2)
    def _(d):
        pre = pre_act[d]
        square = pre * pre
        turned = jnp.tanh(pre * (root + (root * 0.044715) * square))
        gate = 0.5 + 0.5 * turned
        latent[d, 0] = (pre * gate).astype(BF16)
        slope = gate + (0.5 * pre) * (1.0 - turned * turned) * (
            root + (root * 3.0 * 0.044715) * square
        )
        grads[pl.ds(d, grid, stride=pitch), :] = cotangent[d, 0].astype(F32) * slope

    for p in range(channels // 2):
        held_out[pl.ds(p * exchange_rows + x, modes, stride=planes), :] = forward_lines(
            grads[pl.ds(2 * p, grid, stride=pitch), :],
            grads[pl.ds(2 * p + 1, grid, stride=pitch), :],
            z_in[...],
            y_in[...],
        )

    for y in range(grid):
        grad_rows[y * channels : (y + 1) * channels, :] = grads[
            y * pitch : y * pitch + channels, :
        ].astype(BF16)

    @pl.when(x == planes - 1)
    def _():
        for p in range(channels // 2):
            y_modes[:, p * 128 : (p + 1) * 128] = held_out[
                p * exchange_rows : (p + 1) * exchange_rows, :
            ].astype(BF16)


def pull_kernel(
    capacity,
    planes,
    grid,
    base,
    got,
    back,
    grad_rows,
    skip,
    z_out,
    y_out,
    mix_parts,
    point_grads,
    held,
    rows_held,
    total,
    arrived,
):
    channels = point_grads.shape[1]
    pitch = channels + 8
    exchange_rows = back.shape[0]
    modes = exchange_rows // planes
    copy = pltpu.make_async_copy(grad_rows, rows_held, arrived)
    copy.start()
    spread(back, held)

    @pl.loop(0, planes)
    def _(x):
        for p in range(channels // 2):
            values = held[pl.ds(p * exchange_rows + x, modes, stride=planes), :]
            lines = inverse_lines(values, z_out[...], y_out[...])
            for h in range(2):
                start = x * (grid * pitch) + 2 * p + h
                total[pl.ds(start, grid, stride=pitch), :] = lines[:, h * 128 : (h + 1) * 128]

    copy.wait()

    @pl.loop(0, got.shape[0] // capacity)
    def _(i):
        for s in range(capacity):
            block = got[i * capacity + s].astype(F32)
            first = base[i * capacity + s]
            lines = jnp.concatenate(
                [
                    total[pl.ds(pl.multiple_of((first + j) * pitch, 8), channels), :]
                    for j in range(4)
                ],
                axis=0,
            )
            span = pl.ds(pl.multiple_of(first * channels, channels), 4 * channels)
            rows = lines + dot(skip[...], rows_held[span, :])
            near = dot(rows.astype(BF16), near_line_of(block, grid))
            summed = jnp.zeros((channels, 128), F32)
            for j, weight in enumerate(near_rows(block)):
                summed += near[j * channels : (j + 1) * channels] * weight
            point_grads[i * (capacity + 1) + s] = summed.astype(BF16)
        point_grads[i * (capacity + 1) + capacity] = mix_parts[...]


def vmem():
    return pl.BlockSpec(memory_space=pltpu.VMEM)


def params(**more):
    return pltpu.CompilerParams(vmem_limit_bytes=VMEM_BYTES, **more)


def whole(shape):
    return pl.BlockSpec(shape, lambda x: (0,) * len(shape))


def pair_weights(mix):
    channels = mix.shape[0]
    pairs = channels // 2
    cut = mix.reshape(pairs, 2, pairs, 2)
    straight = jnp.stack([cut[:, 0, :, 0], cut[:, 1, :, 1]], axis=-1)
    swapped = jnp.stack([cut[:, 0, :, 1], cut[:, 1, :, 0]], axis=-1)
    both = jnp.stack([straight, swapped], axis=2).reshape(pairs, channels, 2)
    return jnp.repeat(both, 64, axis=-1)


def exchange(values):
    return lax.all_to_all(values, "brick", split_axis=0, concat_axis=0, tiled=True)


def shards(
    point_features,
    point_positions,
    owner_brick,
    block_rows,
    mode_scale,
    channel_mix,
    skip_weight,
    cotangent,
):
    channels, points = point_features.shape
    blocks = points // 128
    planes, grid = cotangent.shape[1], cotangent.shape[2]
    mode_count, own_modes = mode_scale.shape[1], mode_scale.shape[2]
    bricks = lax.axis_size("brick")
    capacity = 3 * blocks // bricks
    slots = bricks * capacity
    local_rows = planes * grid
    width = channels * 2 * mode_count
    exchange_rows = mode_count * planes
    line_rows = grid * channels
    pitch = channels + 8
    pairs = channels // 2
    z_in, y_in, z_out, y_out, x_in, x_out = tables(grid, mode_count, bricks, planes, own_modes)
    share = 1.0 / (grid * grid * grid)

    member = (owner_brick[:, None] == jnp.arange(bricks, dtype=jnp.int32)[None, :]).astype(
        jnp.int32
    )
    earlier = jnp.cumsum(member, axis=0) - member
    target = owner_brick * capacity + jnp.sum(earlier * member, axis=1)
    chosen = (jnp.arange(slots, dtype=jnp.int32)[:, None] == target[None, :]).astype(BF16)
    first_row = jnp.min(block_rows, axis=1)
    plane, along = first_row // grid, first_row % grid
    places = point_positions.reshape(3, blocks, 128)
    dx = (owner_brick * planes + plane).astype(F32)[:, None] - places[0]
    dy = along.astype(F32)[:, None] - places[1]
    cell = jnp.round(places[2])
    dz = places[2] - cell

    def head(values):
        return lax.reduce_precision(values, 8, 7)

    lanes = jnp.arange(128, dtype=jnp.int32)[None, :]
    named = jnp.where(lanes < 64, plane[:, None], along[:, None]).astype(F32)
    extra = jnp.stack(
        [head(dx), dx - head(dx), head(dy), dy - head(dy), cell, head(dz), dz - head(dz), named],
        axis=1,
    ).astype(BF16)
    features = point_features.reshape(channels, blocks, 128).transpose(1, 0, 2)
    sent = jnp.concatenate([features, extra], axis=1)
    sent = jnp.einsum("sb,brp->srp", chosen, sent, preferred_element_type=F32).astype(BF16)
    got = exchange(sent)
    ids = got[:, channels + 7, :].astype(F32).astype(jnp.int32)
    base = jnp.clip(ids[:, 0] * grid + ids[:, 64], 0, local_rows - 4)

    table = lambda values: jnp.asarray(values, BF16)
    smem = pl.BlockSpec(memory_space=pltpu.SMEM)
    encoded, y_modes = pl.pallas_call(
        lambda *refs: encode_kernel(capacity, planes, grid, *refs),
        grid=(planes,),
        in_specs=[smem, whole(got.shape), whole(z_in.shape), whole(y_in.shape)],
        out_specs=[
            pl.BlockSpec((line_rows, 128), lambda x: (x, 0)),
            whole((exchange_rows, width)),
        ],
        out_shape=[
            jax.ShapeDtypeStruct((planes * line_rows, 128), BF16),
            jax.ShapeDtypeStruct((exchange_rows, width), BF16),
        ],
        scratch_shapes=[
            pltpu.VMEM((planes * grid * pitch, 128), F32),
            pltpu.VMEM((pairs * exchange_rows, 128), F32),
        ],
        compiler_params=params(),
        name="encode",
    )(base, got, table(z_in), table(y_in))

    scale = mode_scale.transpose(2, 1, 0, 3).reshape(own_modes * mode_count, width)
    held_modes = pltpu.VMEM((pairs, own_modes * mode_count, 128), F32)
    scaled, back = pl.pallas_call(
        middle_kernel,
        in_specs=[vmem()] * 5,
        out_specs=[vmem()] * 2,
        out_shape=[
            jax.ShapeDtypeStruct(scale.shape, F32),
            jax.ShapeDtypeStruct((exchange_rows, width), BF16),
        ],
        scratch_shapes=[held_modes, held_modes],
        compiler_params=params(),
        name="middle",
    )(exchange(y_modes), table(x_in), table(x_out), scale, pair_weights(channel_mix))

    eye8 = jnp.eye(256 // channels, dtype=BF16)
    eye4 = jnp.eye(4, dtype=BF16)
    planes_spec = pl.BlockSpec((channels, 1, grid, grid), lambda x: (0, x, 0, 0))
    rows_spec = pl.BlockSpec((line_rows, 128), lambda x: (x, 0))
    latent_grid, grad_rows, grad_y_modes = pl.pallas_call(
        lambda *refs: layer_kernel(planes, *refs),
        grid=(planes,),
        in_specs=[
            whole((exchange_rows, width)),
            rows_spec,
            planes_spec,
            whole((256, 256)),
            whole(z_out.shape),
            whole(y_out.shape),
            whole(z_in.shape),
            whole(y_in.shape),
        ],
        out_specs=[planes_spec, rows_spec, whole((exchange_rows, width))],
        out_shape=[
            jax.ShapeDtypeStruct(cotangent.shape, BF16),
            jax.ShapeDtypeStruct((planes * line_rows, 128), BF16),
            jax.ShapeDtypeStruct((exchange_rows, width), BF16),
        ],
        scratch_shapes=[
            pltpu.VMEM((pairs * exchange_rows, 128), F32),
            pltpu.VMEM((grid * pitch, 128), F32),
            pltpu.VMEM((channels, grid, 128), F32),
            pltpu.VMEM((grid * pitch, 128), F32),
            pltpu.VMEM((pairs * exchange_rows, 128), F32),
        ],
        compiler_params=params(),
        name="layer",
    )(
        exchange(back),
        encoded,
        cotangent,
        jnp.kron(eye8, skip_weight),
        table(z_out * share),
        table(y_out),
        table(z_in * share),
        table(y_in),
    )

    grad_back, products = pl.pallas_call(
        middle_grad_kernel,
        in_specs=[vmem()] * 6,
        out_specs=[vmem()] * 2,
        out_shape=[
            jax.ShapeDtypeStruct((exchange_rows, width), BF16),
            jax.ShapeDtypeStruct((2 * pairs * pairs, 128), F32),
        ],
        scratch_shapes=[held_modes, held_modes],
        compiler_params=params(),
        name="middle_grad",
    )(
        exchange(grad_y_modes),
        table(x_in),
        table(x_out),
        scale,
        pair_weights(channel_mix.T),
        scaled,
    )
    by_half = jnp.sum(products.reshape(pairs, pairs, 2, 2, 64), axis=-1)
    by_part = jnp.stack(
        [
            jnp.stack([by_half[:, :, 0, 0], by_half[:, :, 1, 0]], axis=-1),
            jnp.stack([by_half[:, :, 1, 1], by_half[:, :, 0, 1]], axis=-1),
        ],
        axis=2,
    )
    local_mix = by_part.transpose(1, 3, 0, 2).reshape(channels, channels)
    flat_mix = local_mix.reshape(-1, 128)
    first_part = head(flat_mix)
    second_part = head(flat_mix - first_part)
    third_part = flat_mix - first_part - second_part
    mix_parts = jnp.concatenate([first_part, second_part, third_part], axis=0).astype(BF16)
    mix_rows = flat_mix.shape[0]
    mix_parts = jnp.pad(mix_parts, ((0, channels - 3 * mix_rows), (0, 0)))

    pulled = pl.pallas_call(
        lambda *refs: pull_kernel(capacity, planes, grid, *refs),
        in_specs=[smem, vmem(), vmem(), pl.BlockSpec(memory_space=pl.ANY)] + [vmem()] * 4,
        out_specs=vmem(),
        out_shape=jax.ShapeDtypeStruct((slots + bricks, channels, 128), BF16),
        scratch_shapes=[
            pltpu.VMEM((pairs * exchange_rows, 128), F32),
            pltpu.VMEM((planes * line_rows, 128), BF16),
            pltpu.VMEM((planes * grid * pitch, 128), F32),
            pltpu.SemaphoreType.DMA,
        ],
        compiler_params=params(),
        name="pull",
    )(
        base,
        got,
        exchange(grad_back),
        grad_rows,
        jnp.kron(eye4, skip_weight.T),
        table(z_out),
        table(y_out),
        mix_parts,
    )
    returned = exchange(pulled).reshape(bricks, capacity + 1, channels, 128)
    shares = returned[:, capacity, : 3 * mix_rows].astype(F32).reshape(bricks, 3, mix_rows, 128)
    mix_grads = jnp.sum(shares, axis=(0, 1)).reshape(channels, channels) / grid
    returned = returned[:, :capacity].reshape(slots, channels, 128)
    point_grads = jnp.einsum("sb,scp->cbp", chosen, returned, preferred_element_type=F32)
    return (latent_grid, point_grads.astype(BF16).reshape(channels, points), mix_grads)


def solution(mesh):
    in_specs = (
        P(None, ("groups", "brick")),
        P(None, ("groups", "brick")),
        P(("groups", "brick")),
        P(("groups", "brick"), None),
        P(None, None, "brick", None),
        P(),
        P(),
        P(None, ("groups", "brick"), None, None),
    )
    out_specs = (
        P(None, ("groups", "brick"), None, None),
        P(None, ("groups", "brick")),
        P("groups", None),
    )
    return jax.shard_map(shards, mesh=mesh, in_specs=in_specs, out_specs=out_specs, check_vma=False)
```

```python
import math

import jax
import jax.numpy as jnp
import numpy as np
from jax import lax
from jax.experimental import pallas as pl
from jax.experimental.pallas import tpu as pltpu
from jax.sharding import PartitionSpec as P

F32 = jnp.float32
BF16 = jnp.bfloat16
VMEM_BYTES = 56 * 1024 * 1024
PARTS = 2


def rounded(values):
    return np.asarray(values, np.float32).astype(jnp.bfloat16).astype(np.float32)


def tables(grid, modes, bricks, planes, own_modes):
    place = np.arange(grid)
    numbers = np.arange(modes)
    signed = np.where(numbers < modes // 2, numbers, numbers - modes)
    turns = (place[:, None] * signed[None, :] % grid) * (2.0 * math.pi / grid)
    cosine, sine = rounded(np.cos(turns)), rounded(np.sin(turns))
    line_turns = (place[:, None] * numbers[None, :] % grid) * (2.0 * math.pi / grid)
    line = np.stack([np.cos(line_turns), -np.sin(line_turns)], axis=-1)
    line = rounded(line.reshape(grid, 2 * modes))
    turn = np.zeros((2 * modes, 2 * modes), np.float32)
    turn[2 * numbers + 1, 2 * numbers] = 1.0
    turn[2 * numbers, 2 * numbers + 1] = -1.0
    two = np.eye(2, dtype=np.float32)
    z_in = np.concatenate([np.kron(two, line), np.kron(two, line @ turn)], axis=1)
    y_in = np.concatenate([cosine.T, sine.T], axis=1)
    z_out = np.concatenate([np.kron(two, line.T), np.kron(two, turn @ line.T)], axis=1)
    y_out = np.concatenate([cosine, -sine], axis=1)
    x_in = np.zeros((2, own_modes, modes, bricks, own_modes, planes), np.float32)
    x_out = np.zeros((bricks, own_modes, planes, 2, own_modes, modes), np.float32)
    by_brick_cos = cosine.reshape(bricks, planes, modes)
    by_brick_sin = sine.reshape(bricks, planes, modes)
    for k in range(own_modes):
        x_in[0, k, :, :, k, :] = by_brick_cos.transpose(2, 0, 1)
        x_in[1, k, :, :, k, :] = by_brick_sin.transpose(2, 0, 1)
        x_out[:, k, :, 0, k, :] = by_brick_cos
        x_out[:, k, :, 1, k, :] = -by_brick_sin
    part = planes // PARTS
    cuts = [slice(h * part, (h + 1) * part) for h in range(PARTS)]
    x_out_parts = [x_out[:, :, cut].reshape(-1, 2 * own_modes * modes) for cut in cuts]
    x_in_parts = [x_in[..., cut].reshape(2 * own_modes * modes, -1) for cut in cuts]
    return (z_in, y_in, z_out, y_out, x_in.reshape(2 * own_modes * modes, -1), x_in_parts, x_out_parts,
            x_out.reshape(-1, 2 * own_modes * modes))


def dot(left, right):
    return jnp.dot(left, right, preferred_element_type=F32)


def is_even(shape):
    return lax.broadcasted_iota(jnp.int32, shape, 1) % 2 == 0


def rotate(values, even):
    return jnp.where(even, pltpu.roll(values, 127, 1), -pltpu.roll(values, 1, 1))


def near_rows(block):
    dx = block[32:33] + block[33:34]
    dy = block[34:35] + block[35:36]
    return [jnp.exp(-0.5 * (dx * dx + (dy + float(j)) * (dy + float(j)))) for j in range(4)]


def near_line_of(block, grid):
    depth = lax.broadcasted_iota(jnp.int32, (grid, 128), 0).astype(F32)
    away = (depth - block[36:37]) - (block[37:38] + block[38:39])
    return jnp.exp(-0.5 * away * away).astype(BF16)


def forward_lines(first, second, z_in, y_in):
    pair = jnp.concatenate([first.astype(BF16), second.astype(BF16)], axis=1)
    both = dot(pair, z_in).astype(BF16)
    return dot(y_in, jnp.concatenate([both[:, :128], both[:, 128:]], axis=0))


def inverse_lines(values, z_out, y_out):
    both = dot(values.astype(BF16), z_out).astype(BF16)
    return dot(y_out, jnp.concatenate([both[:, :256], both[:, 256:]], axis=0))


def encode_kernel(capacity, planes, grid, base, got, z_in, y_in, encoded, y_modes, total, held):
    x = pl.program_id(0)
    channels = got.shape[1] - 8
    pitch = channels + 8
    modes = y_in.shape[0]
    exchange_rows = modes * planes

    @pl.when(x == 0)
    def _():
        @pl.loop(0, total.shape[0] // 512)
        def _(i):
            total[pl.ds(pl.multiple_of(i * 512, 512), 512), :] = jnp.zeros((512, 128), F32)

        @pl.loop(0, got.shape[0] // capacity)
        def _(i):
            sums = []
            for s in range(capacity):
                block = got[i * capacity + s].astype(F32)
                weighted = jnp.concatenate(
                    [(block[:channels] * near).astype(BF16) for near in near_rows(block)], axis=0
                )
                sums.append(
                    lax.dot_general(
                        weighted,
                        near_line_of(block, grid),
                        (((1,), (1,)), ((), ())),
                        preferred_element_type=F32,
                    )
                )
            for s in range(capacity):
                for j in range(4):
                    start = pl.multiple_of((base[i * capacity + s] + j) * pitch, 8)
                    total[pl.ds(start, channels), :] += sums[s][j * channels : (j + 1) * channels]

    start = pl.multiple_of(x * (grid * pitch), 8)
    for y in range(grid):
        encoded[y * channels : (y + 1) * channels, :] = total[
            pl.ds(start + y * pitch, channels), :
        ].astype(BF16)

    for p in range(channels // 2):
        out = forward_lines(
            total[pl.ds(start + 2 * p, grid, stride=pitch), :],
            total[pl.ds(start + 2 * p + 1, grid, stride=pitch), :],
            z_in[...],
            y_in[...],
        )
        held[pl.ds(p * exchange_rows + x, modes, stride=planes), :] = out

    @pl.when(x == planes - 1)
    def _():
        for p in range(channels // 2):
            y_modes[:, p * 128 : (p + 1) * 128] = held[
                p * exchange_rows : (p + 1) * exchange_rows, :
            ].astype(BF16)


def x_forward(gots, tables_in, even, rows):
    both = sum(dot(x_in[...], got[...]) for got, x_in in zip(gots, tables_in))
    parts = []
    for p in range(both.shape[1] // 128):
        span = slice(p * 128, (p + 1) * 128)
        parts.append(both[:rows, span] + rotate(both[rows:, span], even))
    return parts


def scale_parts(scale, even):
    real = jnp.where(even, scale, pltpu.roll(scale, 1, 1))
    imag = jnp.where(even, pltpu.roll(scale, 127, 1), scale)
    return real, imag


def mix_pairs(d, weights, straight, swapped, pairs):
    total = weights[d, 0:1, :] * straight[0] + weights[d, 1:2, :] * swapped[0]
    for p in range(1, pairs):
        total += weights[d, 2 * p : 2 * p + 1, :] * straight[p]
        total += weights[d, 2 * p + 1 : 2 * p + 2, :] * swapped[p]
    return total


def middle_kernel(got, x_in, *refs):
    x_outs, refs = refs[:PARTS], refs[PARTS:]
    scale, weights, scaled = refs[:3]
    backs, (straight, swapped) = refs[3 : 3 + PARTS], refs[3 + PARTS :]
    rows = scale.shape[0]
    pairs = got.shape[1] // 128
    even = is_even((rows, 128))
    for p, modes in enumerate(x_forward([got], [x_in], even, rows)):
        span = slice(p * 128, (p + 1) * 128)
        real, imag = scale_parts(scale[:, span], even)
        value = modes * real - rotate(modes, even) * imag
        scaled[:, span] = value
        straight[p] = value
        swapped[p] = pltpu.roll(value, 64, 1)
    for d in range(pairs):
        mixed = mix_pairs(d, weights, straight, swapped, pairs)
        stacked = jnp.concatenate([mixed, rotate(mixed, even)], axis=0).astype(BF16)
        for back, x_out in zip(backs, x_outs):
            back[:, d * 128 : (d + 1) * 128] = dot(x_out[...], stacked).astype(BF16)


def middle_grad_kernel(*refs):
    gots, x_ins, refs = refs[:PARTS], refs[PARTS : 2 * PARTS], refs[2 * PARTS :]
    x_out, scale, weights, scaled, back, products, straight, swapped = refs
    rows = scale.shape[0]
    pairs = scale.shape[1] // 128
    even = is_even((rows, 128))
    for p, grad in enumerate(x_forward(gots, x_ins, even, rows)):
        straight[p] = grad
        swapped[p] = pltpu.roll(grad, 64, 1)
    for c in range(pairs):
        span = slice(c * 128, (c + 1) * 128)
        mixed = mix_pairs(c, weights, straight, swapped, pairs)
        real, imag = scale_parts(scale[:, span], even)
        value = mixed * real + rotate(mixed, even) * imag
        stacked = jnp.concatenate([value, rotate(value, even)], axis=0).astype(BF16)
        back[:, span] = dot(x_out[...], stacked).astype(BF16)
    for c in range(pairs):
        value = scaled[:, c * 128 : (c + 1) * 128]
        for d in range(pairs):
            at = (c * pairs + d) * 2
            products[at : at + 1, :] = jnp.sum(value * straight[d], axis=0, keepdims=True)
            products[at + 1 : at + 2, :] = jnp.sum(value * swapped[d], axis=0, keepdims=True)


def spread(got, held):
    rows = got.shape[0]
    for p in range(got.shape[1] // 128):
        held[p * rows : (p + 1) * rows, :] = got[:, p * 128 : (p + 1) * 128].astype(F32)


def layer_kernel(
    planes,
    got,
    encoded,
    cotangent,
    skip,
    z_out,
    y_out,
    z_in,
    y_in,
    _,
    latent,
    grad_rows,
    y_modes,
    held,
    skipped,
    pre_act,
    grads,
    held_out,
):
    x = pl.program_id(0)
    channels, grid = cotangent.shape[0], cotangent.shape[2]
    pitch = channels + 8
    modes = y_in.shape[0]
    exchange_rows = modes * planes

    @pl.when(x == 0)
    def _():
        spread(got, held)

    for g in range(grid * channels // 256):
        mixed = dot(skip[...], encoded[g * 256 : (g + 1) * 256, :])
        for i in range(256 // channels):
            y = g * (256 // channels) + i
            skipped[y * pitch : y * pitch + channels, :] = mixed[i * channels : (i + 1) * channels]

    root = math.sqrt(2.0 / math.pi)

    for p in range(channels // 2):
        values = held[pl.ds(p * exchange_rows + x, modes, stride=planes), :]
        spectral = inverse_lines(values, z_out[...], y_out[...])
        for h in range(2):
            d = 2 * p + h
            mixed = skipped[pl.ds(d, grid, stride=pitch), :]
            pre_act[d] = spectral[:, h * 128 : (h + 1) * 128] + mixed

    @pl.loop(0, channels, unroll=2)
    def _(d):
        pre = pre_act[d]
        square = pre * pre
        turned = jnp.tanh(pre * (root + (root * 0.044715) * square))
        gate = 0.5 + 0.5 * turned
        latent[d, 0] = (pre * gate).astype(BF16)
        slope = gate + (0.5 * pre) * (1.0 - turned * turned) * (
            root + (root * 3.0 * 0.044715) * square
        )
        grads[pl.ds(d, grid, stride=pitch), :] = cotangent[d, 0].astype(F32) * slope

    for p in range(channels // 2):
        held_out[pl.ds(p * exchange_rows + x, modes, stride=planes), :] = forward_lines(
            grads[pl.ds(2 * p, grid, stride=pitch), :],
            grads[pl.ds(2 * p + 1, grid, stride=pitch), :],
            z_in[...],
            y_in[...],
        )

    for y in range(grid):
        grad_rows[y * channels : (y + 1) * channels, :] = grads[
            y * pitch : y * pitch + channels, :
        ].astype(BF16)

    @pl.when(x == planes - 1)
    def _():
        for p in range(channels // 2):
            y_modes[:, p * 128 : (p + 1) * 128] = held_out[
                p * exchange_rows : (p + 1) * exchange_rows, :
            ].astype(BF16)


def pull_kernel(
    capacity,
    planes,
    grid,
    base,
    got,
    back,
    skip,
    z_out,
    y_out,
    mix_parts,
    *refs,
):
    grad_rows, refs = refs[:PARTS], refs[PARTS:]
    point_grads, held, rows_held, total, arrived = refs
    channels = point_grads.shape[1]
    pitch = channels + 8
    exchange_rows = back.shape[0]
    modes = exchange_rows // planes
    part_rows = rows_held.shape[0] // PARTS
    copies = [
        pltpu.make_async_copy(
            part, rows_held.at[h * part_rows : (h + 1) * part_rows], arrived.at[h]
        )
        for h, part in enumerate(grad_rows)
    ]
    for copy in copies:
        copy.start()
    spread(back, held)

    @pl.loop(0, planes)
    def _(x):
        for p in range(channels // 2):
            values = held[pl.ds(p * exchange_rows + x, modes, stride=planes), :]
            lines = inverse_lines(values, z_out[...], y_out[...])
            for h in range(2):
                start = x * (grid * pitch) + 2 * p + h
                total[pl.ds(start, grid, stride=pitch), :] = lines[:, h * 128 : (h + 1) * 128]

    for copy in copies:
        copy.wait()

    @pl.loop(0, got.shape[0] // capacity)
    def _(i):
        for s in range(capacity):
            block = got[i * capacity + s].astype(F32)
            first = base[i * capacity + s]
            lines = jnp.concatenate(
                [
                    total[pl.ds(pl.multiple_of((first + j) * pitch, 8), channels), :]
                    for j in range(4)
                ],
                axis=0,
            )
            span = pl.ds(pl.multiple_of(first * channels, channels), 4 * channels)
            rows = lines + dot(skip[...], rows_held[span, :])
            near = dot(rows.astype(BF16), near_line_of(block, grid))
            summed = jnp.zeros((channels, 128), F32)
            for j, weight in enumerate(near_rows(block)):
                summed += near[j * channels : (j + 1) * channels] * weight
            point_grads[i * (capacity + 1) + s] = summed.astype(BF16)
        point_grads[i * (capacity + 1) + capacity] = mix_parts[...]


def vmem():
    return pl.BlockSpec(memory_space=pltpu.VMEM)


def params(**more):
    return pltpu.CompilerParams(vmem_limit_bytes=VMEM_BYTES, **more)


def whole(shape):
    return pl.BlockSpec(shape, lambda x: (0,) * len(shape))


def pair_weights(mix):
    channels = mix.shape[0]
    pairs = channels // 2
    cut = mix.reshape(pairs, 2, pairs, 2)
    straight = jnp.stack([cut[:, 0, :, 0], cut[:, 1, :, 1]], axis=-1)
    swapped = jnp.stack([cut[:, 0, :, 1], cut[:, 1, :, 0]], axis=-1)
    both = jnp.stack([straight, swapped], axis=2).reshape(pairs, channels, 2)
    return jnp.repeat(both, 64, axis=-1)


def exchange(values):
    return lax.all_to_all(values, "brick", split_axis=0, concat_axis=0, tiled=True)


def shards(
    point_features,
    point_positions,
    owner_brick,
    block_rows,
    mode_scale,
    channel_mix,
    skip_weight,
    cotangent,
):
    channels, points = point_features.shape
    blocks = points // 128
    planes, grid = cotangent.shape[1], cotangent.shape[2]
    mode_count, own_modes = mode_scale.shape[1], mode_scale.shape[2]
    bricks = lax.axis_size("brick")
    capacity = 3 * blocks // bricks
    slots = bricks * capacity
    local_rows = planes * grid
    width = channels * 2 * mode_count
    exchange_rows = mode_count * planes
    line_rows = grid * channels
    pitch = channels + 8
    pairs = channels // 2
    z_in, y_in, z_out, y_out, x_in, x_in_parts, x_out_parts, x_out = tables(grid, mode_count, bricks, planes, own_modes)
    share = 1.0 / (grid * grid * grid)

    member = (owner_brick[:, None] == jnp.arange(bricks, dtype=jnp.int32)[None, :]).astype(
        jnp.int32
    )
    earlier = jnp.cumsum(member, axis=0) - member
    target = owner_brick * capacity + jnp.sum(earlier * member, axis=1)
    chosen = (jnp.arange(slots, dtype=jnp.int32)[:, None] == target[None, :]).astype(BF16)
    first_row = jnp.min(block_rows, axis=1)
    plane, along = first_row // grid, first_row % grid
    places = point_positions.reshape(3, blocks, 128)
    dx = (owner_brick * planes + plane).astype(F32)[:, None] - places[0]
    dy = along.astype(F32)[:, None] - places[1]
    cell = jnp.round(places[2])
    dz = places[2] - cell

    def head(values):
        return lax.reduce_precision(values, 8, 7)

    lanes = jnp.arange(128, dtype=jnp.int32)[None, :]
    named = jnp.where(lanes < 64, plane[:, None], along[:, None]).astype(F32)
    extra = jnp.stack(
        [head(dx), dx - head(dx), head(dy), dy - head(dy), cell, head(dz), dz - head(dz), named],
        axis=1,
    ).astype(BF16)
    features = point_features.reshape(channels, blocks, 128).transpose(1, 0, 2)
    sent = jnp.concatenate([features, extra], axis=1)
    sent = jnp.einsum("sb,brp->srp", chosen, sent, preferred_element_type=F32).astype(BF16)
    got = exchange(sent)
    ids = got[:, channels + 7, :].astype(F32).astype(jnp.int32)
    base = jnp.clip(ids[:, 0] * grid + ids[:, 64], 0, local_rows - 4)

    table = lambda values: jnp.asarray(values, BF16)
    smem = pl.BlockSpec(memory_space=pltpu.SMEM)
    encoded, y_modes = pl.pallas_call(
        lambda *refs: encode_kernel(capacity, planes, grid, *refs),
        grid=(planes,),
        in_specs=[smem, whole(got.shape), whole(z_in.shape), whole(y_in.shape)],
        out_specs=[
            pl.BlockSpec((line_rows, 128), lambda x: (x, 0)),
            whole((exchange_rows, width)),
        ],
        out_shape=[
            jax.ShapeDtypeStruct((planes * line_rows, 128), BF16),
            jax.ShapeDtypeStruct((exchange_rows, width), BF16),
        ],
        scratch_shapes=[
            pltpu.VMEM((planes * grid * pitch, 128), F32),
            pltpu.VMEM((pairs * exchange_rows, 128), F32),
        ],
        compiler_params=params(),
        name="encode",
    )(base, got, table(z_in), table(y_in))

    scale = mode_scale.transpose(2, 1, 0, 3).reshape(own_modes * mode_count, width)
    held_modes = pltpu.VMEM((pairs, own_modes * mode_count, 128), F32)
    part_rows = exchange_rows // PARTS
    half_modes = jax.ShapeDtypeStruct((part_rows, width), BF16)
    scaled, *backs = pl.pallas_call(
        middle_kernel,
        in_specs=[vmem()] * (4 + PARTS),
        out_specs=[vmem()] * (1 + PARTS),
        out_shape=[jax.ShapeDtypeStruct(scale.shape, F32)] + [half_modes] * PARTS,
        scratch_shapes=[held_modes, held_modes],
        compiler_params=params(),
        name="middle",
    )(
        exchange(y_modes),
        table(x_in),
        *[table(values) for values in x_out_parts],
        scale,
        pair_weights(channel_mix),
    )

    eye8 = jnp.eye(256 // channels, dtype=BF16)
    eye4 = jnp.eye(4, dtype=BF16)
    part_planes = planes // PARTS
    skip_blocks = jnp.kron(eye8, skip_weight)
    layer_cost = pl.CostEstimate(
        flops=40 * channels * part_planes * grid * grid,
        bytes_accessed=16 * channels * part_planes * grid * grid,
        transcendentals=channels * part_planes * grid * grid,
    )
    latent_grid = None
    grad_rows, grad_y_modes = [], []
    for part in range(PARTS):
        first = part * part_planes
        planes_spec = pl.BlockSpec(
            (channels, 1, grid, grid), lambda x, first=first: (0, first + x, 0, 0)
        )
        rows_in = pl.BlockSpec((line_rows, 128), lambda x, first=first: (first + x, 0))
        rows_out = pl.BlockSpec((line_rows, 128), lambda x: (x, 0))
        latent_grid, rows_part, modes_part = pl.pallas_call(
            lambda *refs: layer_kernel(part_planes, *refs),
            grid=(part_planes,),
            in_specs=[
                whole((part_rows, width)),
                rows_in,
                planes_spec,
                whole((256, 256)),
                whole(z_out.shape),
                whole(y_out.shape),
                whole(z_in.shape),
                whole(y_in.shape),
                pl.BlockSpec(memory_space=pl.ANY),
            ],
            out_specs=[planes_spec, rows_out, whole((part_rows, width))],
            out_shape=[
                jax.ShapeDtypeStruct(cotangent.shape, BF16),
                jax.ShapeDtypeStruct((part_planes * line_rows, 128), BF16),
                half_modes,
            ],
            scratch_shapes=[
                pltpu.VMEM((pairs * part_rows, 128), F32),
                pltpu.VMEM((grid * pitch, 128), F32),
                pltpu.VMEM((channels, grid, 128), F32),
                pltpu.VMEM((grid * pitch, 128), F32),
                pltpu.VMEM((pairs * part_rows, 128), F32),
            ],
            input_output_aliases={} if latent_grid is None else {8: 0},
            cost_estimate=layer_cost,
            compiler_params=params(),
            name="layer",
        )(
            exchange(backs[part]),
            encoded,
            cotangent,
            skip_blocks,
            table(z_out * share),
            table(y_out),
            table(z_in * share),
            table(y_in),
            encoded if latent_grid is None else latent_grid,
        )
        grad_rows.append(rows_part)
        grad_y_modes.append(modes_part)

    grad_back, products = pl.pallas_call(
        middle_grad_kernel,
        in_specs=[vmem()] * (4 + 2 * PARTS),
        out_specs=[vmem()] * 2,
        out_shape=[
            jax.ShapeDtypeStruct((exchange_rows, width), BF16),
            jax.ShapeDtypeStruct((2 * pairs * pairs, 128), F32),
        ],
        scratch_shapes=[held_modes, held_modes],
        compiler_params=params(),
        name="middle_grad",
    )(
        *[exchange(values) for values in grad_y_modes],
        *[table(values) for values in x_in_parts],
        table(x_out),
        scale,
        pair_weights(channel_mix.T),
        scaled,
    )
    by_half = jnp.sum(products.reshape(pairs, pairs, 2, 2, 64), axis=-1)
    by_part = jnp.stack(
        [
            jnp.stack([by_half[:, :, 0, 0], by_half[:, :, 1, 0]], axis=-1),
            jnp.stack([by_half[:, :, 1, 1], by_half[:, :, 0, 1]], axis=-1),
        ],
        axis=2,
    )
    local_mix = by_part.transpose(1, 3, 0, 2).reshape(channels, channels)
    flat_mix = local_mix.reshape(-1, 128)
    first_part = head(flat_mix)
    second_part = head(flat_mix - first_part)
    third_part = flat_mix - first_part - second_part
    mix_parts = jnp.concatenate([first_part, second_part, third_part], axis=0).astype(BF16)
    mix_rows = flat_mix.shape[0]
    mix_parts = jnp.pad(mix_parts, ((0, channels - 3 * mix_rows), (0, 0)))

    pulled = pl.pallas_call(
        lambda *refs: pull_kernel(capacity, planes, grid, *refs),
        in_specs=[smem] + [vmem()] * 6 + [pl.BlockSpec(memory_space=pl.ANY)] * PARTS,
        out_specs=vmem(),
        out_shape=jax.ShapeDtypeStruct((slots + bricks, channels, 128), BF16),
        scratch_shapes=[
            pltpu.VMEM((pairs * exchange_rows, 128), F32),
            pltpu.VMEM((planes * line_rows, 128), BF16),
            pltpu.VMEM((planes * grid * pitch, 128), F32),
            pltpu.SemaphoreType.DMA((PARTS,)),
        ],
        compiler_params=params(),
        name="pull",
    )(
        base,
        got,
        exchange(grad_back),
        jnp.kron(eye4, skip_weight.T),
        table(z_out),
        table(y_out),
        mix_parts,
        *grad_rows,
    )
    returned = exchange(pulled).reshape(bricks, capacity + 1, channels, 128)
    shares = returned[:, capacity, : 3 * mix_rows].astype(F32).reshape(bricks, 3, mix_rows, 128)
    mix_grads = jnp.sum(shares, axis=(0, 1)).reshape(channels, channels) / grid
    returned = returned[:, :capacity].reshape(slots, channels, 128)
    point_grads = jnp.einsum("sb,scp->cbp", chosen, returned, preferred_element_type=F32)
    return (latent_grid, point_grads.astype(BF16).reshape(channels, points), mix_grads)


def solution(mesh):
    in_specs = (
        P(None, ("groups", "brick")),
        P(None, ("groups", "brick")),
        P(("groups", "brick")),
        P(("groups", "brick"), None),
        P(None, None, "brick", None),
        P(),
        P(),
        P(None, ("groups", "brick"), None, None),
    )
    out_specs = (
        P(None, ("groups", "brick"), None, None),
        P(None, ("groups", "brick")),
        P("groups", None),
    )
    return jax.shard_map(shards, mesh=mesh, in_specs=in_specs, out_specs=out_specs, check_vma=False)
```

```python
import math

import jax
import jax.numpy as jnp
import numpy as np
from jax import lax
from jax.experimental import pallas as pl
from jax.experimental.pallas import tpu as pltpu
from jax.sharding import PartitionSpec as P

F32 = jnp.float32
BF16 = jnp.bfloat16
VMEM_BYTES = 56 * 1024 * 1024


def rounded(values):
    return np.asarray(values, np.float32).astype(jnp.bfloat16).astype(np.float32)


def tables(grid, modes, bricks, planes, own_modes):
    place = np.arange(grid)
    numbers = np.arange(modes)
    signed = np.where(numbers < modes // 2, numbers, numbers - modes)
    turns = (place[:, None] * signed[None, :] % grid) * (2.0 * math.pi / grid)
    cosine, sine = rounded(np.cos(turns)), rounded(np.sin(turns))
    line_turns = (place[:, None] * numbers[None, :] % grid) * (2.0 * math.pi / grid)
    line = np.stack([np.cos(line_turns), -np.sin(line_turns)], axis=-1)
    line = rounded(line.reshape(grid, 2 * modes))
    turn = np.zeros((2 * modes, 2 * modes), np.float32)
    turn[2 * numbers + 1, 2 * numbers] = 1.0
    turn[2 * numbers, 2 * numbers + 1] = -1.0
    two = np.eye(2, dtype=np.float32)
    z_in = np.kron(two, np.concatenate([line, line @ turn], axis=0))
    y_in = np.concatenate([cosine.T, sine.T], axis=0)
    z_out = np.concatenate([np.kron(two, line.T), np.kron(two, turn @ line.T)], axis=1)
    y_out = np.concatenate([cosine, -sine], axis=1)
    x_in = np.zeros((2, own_modes, modes, bricks, own_modes, planes), np.float32)
    x_out = np.zeros((bricks, own_modes, planes, 2, own_modes, modes), np.float32)
    by_brick_cos = cosine.reshape(bricks, planes, modes)
    by_brick_sin = sine.reshape(bricks, planes, modes)
    for k in range(own_modes):
        x_in[0, k, :, :, k, :] = by_brick_cos.transpose(2, 0, 1)
        x_in[1, k, :, :, k, :] = by_brick_sin.transpose(2, 0, 1)
        x_out[:, k, :, 0, k, :] = by_brick_cos
        x_out[:, k, :, 1, k, :] = -by_brick_sin
    rows = bricks * own_modes * planes
    x_in = x_in.reshape(2 * own_modes * modes, rows)
    x_out = x_out.reshape(rows, 2 * own_modes * modes)
    return z_in, y_in, z_out, y_out, x_in, x_out


def dot(left, right):
    return jnp.dot(left, right, preferred_element_type=F32)


def is_even(shape):
    return lax.broadcasted_iota(jnp.int32, shape, 1) % 2 == 0


def rotate(values, even):
    return jnp.where(even, pltpu.roll(values, 127, 1), -pltpu.roll(values, 1, 1))


def near_rows(block):
    dx = block[32:33] + block[33:34]
    dy = block[34:35] + block[35:36]
    return [jnp.exp(-0.5 * (dx * dx + (dy + float(j)) * (dy + float(j)))) for j in range(4)]


def near_line_of(block, grid):
    depth = lax.broadcasted_iota(jnp.int32, (grid, 128), 0).astype(F32)
    away = (depth - block[36:37]) - (block[37:38] + block[38:39])
    return jnp.exp(-0.5 * away * away).astype(BF16)


def forward_lines(lines_of, channels, z_in, y_in):
    modes = y_in.shape[0] // 2
    wide = []
    for p in range(channels // 2):
        pair = jnp.concatenate([lines_of(2 * p).astype(BF16), lines_of(2 * p + 1).astype(BF16)], axis=1)
        turned = dot(y_in, pair).astype(BF16)
        cosine, sine = turned[:modes], turned[modes:]
        wide.append(
            jnp.concatenate([cosine[:, :128], sine[:, :128], cosine[:, 128:], sine[:, 128:]], axis=1)
        )
    return dot(jnp.concatenate(wide, axis=0), z_in)


def inverse_lines(values_of, channels, modes, z_out, y_out):
    values = jnp.concatenate([values_of(p).astype(BF16) for p in range(channels // 2)], axis=0)
    both = dot(values, z_out).astype(BF16)
    for p in range(channels // 2):
        rows = both[p * modes : (p + 1) * modes]
        yield p, dot(y_out, jnp.concatenate([rows[:, :256], rows[:, 256:]], axis=0))


def encode_kernel(capacity, planes, grid, base, got, z_in, y_in, encoded, y_modes, total, held):
    x = pl.program_id(0)
    channels = got.shape[1] - 8
    pitch = channels + 8
    modes = y_in.shape[0] // 2
    exchange_rows = modes * planes

    @pl.when(x == 0)
    def _():
        @pl.loop(0, total.shape[0] // 512)
        def _(i):
            total[pl.ds(pl.multiple_of(i * 512, 512), 512), :] = jnp.zeros((512, 128), F32)

        @pl.loop(0, got.shape[0] // capacity)
        def _(i):
            sums = []
            for s in range(capacity):
                block = got[i * capacity + s].astype(F32)
                weighted = jnp.concatenate(
                    [(block[:channels] * near).astype(BF16) for near in near_rows(block)], axis=0
                )
                sums.append(
                    lax.dot_general(
                        weighted,
                        near_line_of(block, grid),
                        (((1,), (1,)), ((), ())),
                        preferred_element_type=F32,
                    )
                )
            for s in range(capacity):
                for j in range(4):
                    start = pl.multiple_of((base[i * capacity + s] + j) * pitch, 8)
                    total[pl.ds(start, channels), :] += sums[s][j * channels : (j + 1) * channels]

    start = pl.multiple_of(x * (grid * pitch), 8)
    for y in range(grid):
        encoded[y * channels : (y + 1) * channels, :] = total[
            pl.ds(start + y * pitch, channels), :
        ].astype(BF16)

    out = forward_lines(
        lambda c: total[pl.ds(start + c, grid, stride=pitch), :], channels, z_in[...], y_in[...]
    )
    for p in range(channels // 2):
        held[pl.ds(p * exchange_rows + x, modes, stride=planes), :] = out[
            p * modes : (p + 1) * modes
        ]

    @pl.when(x == planes - 1)
    def _():
        for p in range(channels // 2):
            y_modes[:, p * 128 : (p + 1) * 128] = held[
                p * exchange_rows : (p + 1) * exchange_rows, :
            ].astype(BF16)


def x_forward(got, x_in, even, rows):
    both = dot(x_in[...], got[...])
    parts = []
    for p in range(got.shape[1] // 128):
        span = slice(p * 128, (p + 1) * 128)
        parts.append(both[:rows, span] + rotate(both[rows:, span], even))
    return parts


def scale_parts(scale, even):
    real = jnp.where(even, scale, pltpu.roll(scale, 1, 1))
    imag = jnp.where(even, pltpu.roll(scale, 127, 1), scale)
    return real, imag


def mix_pairs(d, weights, straight, swapped, pairs):
    total = weights[d, 0:1, :] * straight[0] + weights[d, 1:2, :] * swapped[0]
    for p in range(1, pairs):
        total += weights[d, 2 * p : 2 * p + 1, :] * straight[p]
        total += weights[d, 2 * p + 1 : 2 * p + 2, :] * swapped[p]
    return total


def middle_kernel(got, x_in, x_out, scale, weights, scaled, back, straight, swapped):
    rows = scale.shape[0]
    pairs = got.shape[1] // 128
    even = is_even((rows, 128))
    for p, modes in enumerate(x_forward(got, x_in, even, rows)):
        span = slice(p * 128, (p + 1) * 128)
        real, imag = scale_parts(scale[:, span], even)
        value = modes * real - rotate(modes, even) * imag
        scaled[:, span] = value
        straight[p] = value
        swapped[p] = pltpu.roll(value, 64, 1)
    for d in range(pairs):
        mixed = mix_pairs(d, weights, straight, swapped, pairs)
        stacked = jnp.concatenate([mixed, rotate(mixed, even)], axis=0).astype(BF16)
        back[:, d * 128 : (d + 1) * 128] = dot(x_out[...], stacked).astype(BF16)


def middle_grad_kernel(
    got, x_in, x_out, scale, weights, scaled, back, products, straight, swapped
):
    rows = scale.shape[0]
    pairs = got.shape[1] // 128
    even = is_even((rows, 128))
    for p, grad in enumerate(x_forward(got, x_in, even, rows)):
        straight[p] = grad
        swapped[p] = pltpu.roll(grad, 64, 1)
    for c in range(pairs):
        span = slice(c * 128, (c + 1) * 128)
        mixed = mix_pairs(c, weights, straight, swapped, pairs)
        real, imag = scale_parts(scale[:, span], even)
        value = mixed * real + rotate(mixed, even) * imag
        stacked = jnp.concatenate([value, rotate(value, even)], axis=0).astype(BF16)
        back[:, span] = dot(x_out[...], stacked).astype(BF16)
    for c in range(pairs):
        value = scaled[:, c * 128 : (c + 1) * 128]
        for d in range(pairs):
            at = (c * pairs + d) * 2
            products[at : at + 1, :] = jnp.sum(value * straight[d], axis=0, keepdims=True)
            products[at + 1 : at + 2, :] = jnp.sum(value * swapped[d], axis=0, keepdims=True)


def spread(got, held):
    rows = got.shape[0]
    for p in range(got.shape[1] // 128):
        held[p * rows : (p + 1) * rows, :] = got[:, p * 128 : (p + 1) * 128].astype(F32)


def layer_kernel(
    planes,
    got,
    encoded,
    cotangent,
    skip,
    z_out,
    y_out,
    z_in,
    y_in,
    latent,
    grad_rows,
    y_modes,
    held,
    skipped,
    pre_act,
    grads,
    held_out,
):
    x = pl.program_id(0)
    channels, grid = cotangent.shape[0], cotangent.shape[2]
    pitch = channels + 8
    modes = y_in.shape[0] // 2
    exchange_rows = modes * planes

    @pl.when(x == 0)
    def _():
        spread(got, held)

    for g in range(grid * channels // 256):
        mixed = dot(skip[...], encoded[g * 256 : (g + 1) * 256, :])
        for i in range(256 // channels):
            y = g * (256 // channels) + i
            skipped[y * pitch : y * pitch + channels, :] = mixed[i * channels : (i + 1) * channels]

    root = math.sqrt(2.0 / math.pi)

    def values_of(p):
        return held[pl.ds(p * exchange_rows + x, modes, stride=planes), :]

    for p, spectral in inverse_lines(values_of, channels, modes, z_out[...], y_out[...]):
        for h in range(2):
            d = 2 * p + h
            mixed = skipped[pl.ds(d, grid, stride=pitch), :]
            pre_act[d] = spectral[:, h * 128 : (h + 1) * 128] + mixed

    @pl.loop(0, channels, unroll=32)
    def _(d):
        pre = pre_act[d]
        square = pre * pre
        turned = jnp.tanh(pre * (root + (root * 0.044715) * square))
        gate = 0.5 + 0.5 * turned
        latent[d, 0] = (pre * gate).astype(BF16)
        slope = gate + (0.5 * pre) * (1.0 - turned * turned) * (
            root + (root * 3.0 * 0.044715) * square
        )
        grads[pl.ds(d, grid, stride=pitch), :] = cotangent[d, 0].astype(F32) * slope

    out = forward_lines(
        lambda c: grads[pl.ds(c, grid, stride=pitch), :], channels, z_in[...], y_in[...]
    )
    for p in range(channels // 2):
        held_out[pl.ds(p * exchange_rows + x, modes, stride=planes), :] = out[
            p * modes : (p + 1) * modes
        ]

    for y in range(grid):
        grad_rows[y * channels : (y + 1) * channels, :] = grads[
            y * pitch : y * pitch + channels, :
        ].astype(BF16)

    @pl.when(x == planes - 1)
    def _():
        for p in range(channels // 2):
            y_modes[:, p * 128 : (p + 1) * 128] = held_out[
                p * exchange_rows : (p + 1) * exchange_rows, :
            ].astype(BF16)


def pull_kernel(
    capacity,
    planes,
    grid,
    base,
    got,
    back,
    grad_rows,
    skip,
    z_out,
    y_out,
    mix_parts,
    point_grads,
    held,
    rows_held,
    total,
    arrived,
):
    channels = point_grads.shape[1]
    pitch = channels + 8
    exchange_rows = back.shape[0]
    modes = exchange_rows // planes
    copy = pltpu.make_async_copy(grad_rows, rows_held, arrived)
    copy.start()
    spread(back, held)

    @pl.loop(0, planes)
    def _(x):
        def values_of(p):
            return held[pl.ds(p * exchange_rows + x, modes, stride=planes), :]

        for p, lines in inverse_lines(values_of, channels, modes, z_out[...], y_out[...]):
            for h in range(2):
                start = x * (grid * pitch) + 2 * p + h
                total[pl.ds(start, grid, stride=pitch), :] = lines[:, h * 128 : (h + 1) * 128]

    copy.wait()

    @pl.loop(0, got.shape[0] // capacity)
    def _(i):
        for s in range(capacity):
            block = got[i * capacity + s].astype(F32)
            first = base[i * capacity + s]
            lines = jnp.concatenate(
                [
                    total[pl.ds(pl.multiple_of((first + j) * pitch, 8), channels), :]
                    for j in range(4)
                ],
                axis=0,
            )
            span = pl.ds(pl.multiple_of(first * channels, channels), 4 * channels)
            rows = lines + dot(skip[...], rows_held[span, :])
            near = dot(rows.astype(BF16), near_line_of(block, grid))
            summed = jnp.zeros((channels, 128), F32)
            for j, weight in enumerate(near_rows(block)):
                summed += near[j * channels : (j + 1) * channels] * weight
            point_grads[i * (capacity + 1) + s] = summed.astype(BF16)
        point_grads[i * (capacity + 1) + capacity] = mix_parts[...]


def vmem():
    return pl.BlockSpec(memory_space=pltpu.VMEM)


def params(**more):
    return pltpu.CompilerParams(vmem_limit_bytes=VMEM_BYTES, **more)


def whole(shape):
    return pl.BlockSpec(shape, lambda x: (0,) * len(shape))


def pair_weights(mix):
    channels = mix.shape[0]
    pairs = channels // 2
    cut = mix.reshape(pairs, 2, pairs, 2)
    straight = jnp.stack([cut[:, 0, :, 0], cut[:, 1, :, 1]], axis=-1)
    swapped = jnp.stack([cut[:, 0, :, 1], cut[:, 1, :, 0]], axis=-1)
    both = jnp.stack([straight, swapped], axis=2).reshape(pairs, channels, 2)
    return jnp.repeat(both, 64, axis=-1)


def exchange(values):
    return lax.all_to_all(values, "brick", split_axis=0, concat_axis=0, tiled=True)


def shards(
    point_features,
    point_positions,
    owner_brick,
    block_rows,
    mode_scale,
    channel_mix,
    skip_weight,
    cotangent,
):
    channels, points = point_features.shape
    blocks = points // 128
    planes, grid = cotangent.shape[1], cotangent.shape[2]
    mode_count, own_modes = mode_scale.shape[1], mode_scale.shape[2]
    bricks = lax.axis_size("brick")
    capacity = 3 * blocks // bricks
    slots = bricks * capacity
    local_rows = planes * grid
    width = channels * 2 * mode_count
    exchange_rows = mode_count * planes
    line_rows = grid * channels
    pitch = channels + 8
    pairs = channels // 2
    z_in, y_in, z_out, y_out, x_in, x_out = tables(grid, mode_count, bricks, planes, own_modes)
    share = 1.0 / (grid * grid * grid)

    member = (owner_brick[:, None] == jnp.arange(bricks, dtype=jnp.int32)[None, :]).astype(
        jnp.int32
    )
    earlier = jnp.cumsum(member, axis=0) - member
    target = owner_brick * capacity + jnp.sum(earlier * member, axis=1)
    chosen = (jnp.arange(slots, dtype=jnp.int32)[:, None] == target[None, :]).astype(BF16)
    first_row = jnp.min(block_rows, axis=1)
    plane, along = first_row // grid, first_row % grid
    places = point_positions.reshape(3, blocks, 128)
    dx = (owner_brick * planes + plane).astype(F32)[:, None] - places[0]
    dy = along.astype(F32)[:, None] - places[1]
    cell = jnp.round(places[2])
    dz = places[2] - cell

    def head(values):
        return lax.reduce_precision(values, 8, 7)

    lanes = jnp.arange(128, dtype=jnp.int32)[None, :]
    named = jnp.where(lanes < 64, plane[:, None], along[:, None]).astype(F32)
    extra = jnp.stack(
        [head(dx), dx - head(dx), head(dy), dy - head(dy), cell, head(dz), dz - head(dz), named],
        axis=1,
    ).astype(BF16)
    features = point_features.reshape(channels, blocks, 128).transpose(1, 0, 2)
    sent = jnp.concatenate([features, extra], axis=1)
    sent = jnp.einsum("sb,brp->srp", chosen, sent, preferred_element_type=F32).astype(BF16)
    got = exchange(sent)
    ids = got[:, channels + 7, :].astype(F32).astype(jnp.int32)
    base = jnp.clip(ids[:, 0] * grid + ids[:, 64], 0, local_rows - 4)

    table = lambda values: jnp.asarray(values, BF16)
    smem = pl.BlockSpec(memory_space=pltpu.SMEM)
    encoded, y_modes = pl.pallas_call(
        lambda *refs: encode_kernel(capacity, planes, grid, *refs),
        grid=(planes,),
        in_specs=[smem, whole(got.shape), whole(z_in.shape), whole(y_in.shape)],
        out_specs=[
            pl.BlockSpec((line_rows, 128), lambda x: (x, 0)),
            whole((exchange_rows, width)),
        ],
        out_shape=[
            jax.ShapeDtypeStruct((planes * line_rows, 128), BF16),
            jax.ShapeDtypeStruct((exchange_rows, width), BF16),
        ],
        scratch_shapes=[
            pltpu.VMEM((planes * grid * pitch, 128), F32),
            pltpu.VMEM((pairs * exchange_rows, 128), F32),
        ],
        compiler_params=params(),
        name="encode",
    )(base, got, table(z_in), table(y_in))

    scale = mode_scale.transpose(2, 1, 0, 3).reshape(own_modes * mode_count, width)
    held_modes = pltpu.VMEM((pairs, own_modes * mode_count, 128), F32)
    scaled, back = pl.pallas_call(
        middle_kernel,
        in_specs=[vmem()] * 5,
        out_specs=[vmem()] * 2,
        out_shape=[
            jax.ShapeDtypeStruct(scale.shape, F32),
            jax.ShapeDtypeStruct((exchange_rows, width), BF16),
        ],
        scratch_shapes=[held_modes, held_modes],
        compiler_params=params(),
        name="middle",
    )(exchange(y_modes), table(x_in), table(x_out), scale, pair_weights(channel_mix))

    eye8 = jnp.eye(256 // channels, dtype=BF16)
    eye4 = jnp.eye(4, dtype=BF16)
    planes_spec = pl.BlockSpec((channels, 1, grid, grid), lambda x: (0, x, 0, 0))
    rows_spec = pl.BlockSpec((line_rows, 128), lambda x: (x, 0))
    latent_grid, grad_rows, grad_y_modes = pl.pallas_call(
        lambda *refs: layer_kernel(planes, *refs),
        grid=(planes,),
        in_specs=[
            whole((exchange_rows, width)),
            rows_spec,
            planes_spec,
            whole((256, 256)),
            whole(z_out.shape),
            whole(y_out.shape),
            whole(z_in.shape),
            whole(y_in.shape),
        ],
        out_specs=[planes_spec, rows_spec, whole((exchange_rows, width))],
        out_shape=[
            jax.ShapeDtypeStruct(cotangent.shape, BF16),
            jax.ShapeDtypeStruct((planes * line_rows, 128), BF16),
            jax.ShapeDtypeStruct((exchange_rows, width), BF16),
        ],
        scratch_shapes=[
            pltpu.VMEM((pairs * exchange_rows, 128), F32),
            pltpu.VMEM((grid * pitch, 128), F32),
            pltpu.VMEM((channels, grid, 128), F32),
            pltpu.VMEM((grid * pitch, 128), F32),
            pltpu.VMEM((pairs * exchange_rows, 128), F32),
        ],
        compiler_params=params(),
        name="layer",
    )(
        exchange(back),
        encoded,
        cotangent,
        jnp.kron(eye8, skip_weight),
        table(z_out * share),
        table(y_out),
        table(z_in * share),
        table(y_in),
    )

    grad_back, products = pl.pallas_call(
        middle_grad_kernel,
        in_specs=[vmem()] * 6,
        out_specs=[vmem()] * 2,
        out_shape=[
            jax.ShapeDtypeStruct((exchange_rows, width), BF16),
            jax.ShapeDtypeStruct((2 * pairs * pairs, 128), F32),
        ],
        scratch_shapes=[held_modes, held_modes],
        compiler_params=params(),
        name="middle_grad",
    )(
        exchange(grad_y_modes),
        table(x_in),
        table(x_out),
        scale,
        pair_weights(channel_mix.T),
        scaled,
    )
    by_half = jnp.sum(products.reshape(pairs, pairs, 2, 2, 64), axis=-1)
    by_part = jnp.stack(
        [
            jnp.stack([by_half[:, :, 0, 0], by_half[:, :, 1, 0]], axis=-1),
            jnp.stack([by_half[:, :, 1, 1], by_half[:, :, 0, 1]], axis=-1),
        ],
        axis=2,
    )
    local_mix = by_part.transpose(1, 3, 0, 2).reshape(channels, channels)
    flat_mix = local_mix.reshape(-1, 128)
    first_part = head(flat_mix)
    second_part = head(flat_mix - first_part)
    third_part = flat_mix - first_part - second_part
    mix_parts = jnp.concatenate([first_part, second_part, third_part], axis=0).astype(BF16)
    mix_rows = flat_mix.shape[0]
    mix_parts = jnp.pad(mix_parts, ((0, channels - 3 * mix_rows), (0, 0)))

    pulled = pl.pallas_call(
        lambda *refs: pull_kernel(capacity, planes, grid, *refs),
        in_specs=[smem, vmem(), vmem(), pl.BlockSpec(memory_space=pl.ANY)] + [vmem()] * 4,
        out_specs=vmem(),
        out_shape=jax.ShapeDtypeStruct((slots + bricks, channels, 128), BF16),
        scratch_shapes=[
            pltpu.VMEM((pairs * exchange_rows, 128), F32),
            pltpu.VMEM((planes * line_rows, 128), BF16),
            pltpu.VMEM((planes * grid * pitch, 128), F32),
            pltpu.SemaphoreType.DMA,
        ],
        compiler_params=params(),
        name="pull",
    )(
        base,
        got,
        exchange(grad_back),
        grad_rows,
        jnp.kron(eye4, skip_weight.T),
        table(z_out),
        table(y_out),
        mix_parts,
    )
    returned = exchange(pulled).reshape(bricks, capacity + 1, channels, 128)
    shares = returned[:, capacity, : 3 * mix_rows].astype(F32).reshape(bricks, 3, mix_rows, 128)
    mix_grads = jnp.sum(shares, axis=(0, 1)).reshape(channels, channels) / grid
    returned = returned[:, :capacity].reshape(slots, channels, 128)
    point_grads = jnp.einsum("sb,scp->cbp", chosen, returned, preferred_element_type=F32)
    return (latent_grid, point_grads.astype(BF16).reshape(channels, points), mix_grads)


def solution(mesh):
    in_specs = (
        P(None, ("groups", "brick")),
        P(None, ("groups", "brick")),
        P(("groups", "brick")),
        P(("groups", "brick"), None),
        P(None, None, "brick", None),
        P(),
        P(),
        P(None, ("groups", "brick"), None, None),
    )
    out_specs = (
        P(None, ("groups", "brick"), None, None),
        P(None, ("groups", "brick")),
        P("groups", None),
    )
    return jax.shard_map(shards, mesh=mesh, in_specs=in_specs, out_specs=out_specs, check_vma=False)
```
